32 devices in a mesh: req: 16 (over z, y, x), tp: 2 (over core).
Axes of the slice: x: 2, y: 2, z: 4, core: 2. Of those that a mesh axis runs over, the one named last changes fastest.
Arguments:
- attn_heads: bfloat16 [2048, 2048], P('req', 'tp'), may hold values from -6 to 6
- residual_in: bfloat16 [2048, 4096], P('req', 'tp'), may hold values from -45 to 45
- w_out: bfloat16 [2048, 4096], P('tp'), may hold values from -0.125 to 0.125
- gain_attn: float32 [4096], P('tp'), may hold values from 0.1 to 1.9
- router: bfloat16 [4096, 4], P('tp'), may hold values from -0.09375 to 0.09375
- expert_ids: int32 [2048, 2], P('req'), may hold values from 0 to 3, all different within a row; in each aligned block of 64 rows (0 to 63, 64 to 127, ...) at most 48 rows name the same one
- lengths: int32 [16, 5], P('req'), may hold values from 1 to 64, 128 in all within a row
- placement: int32 [8], replicated, may hold values from 0 to 3, as said below
- w_gate_up: bfloat16 [16, 2, 4096, 3584], P('req', None, None, 'tp'), may hold values from -1 to 1, as said below
- w_down: bfloat16 [16, 3584, 4096], P('req', 'tp'), may hold values from -1 to 1, as said below
- gain_final: float32 [4096], P('tp'), may hold values from 0.1 to 1.9
Outputs:
- residual_out: bfloat16 [2048, 4096], P('req', 'tp')
- normed_out: bfloat16 [2048, 4096], P('req', 'tp')
The draws below stay inside these ranges and needn't reach their ends.
Inputs may be any that keep to these rules, and one draw needn't show every extreme that they name: `expert_ids`: in each aligned block of 64 rows no expert is named by more than 48 rows, and the two experts of a row differ. `placement`: every expert is held by exactly two pairs. `w_gate_up`: index 2 s + h holds the h-th half of the hidden units of expert placement[s]; the two pairs of one expert hold equal values. `w_down`: index 2 s + h holds the h-th half of the hidden units of expert placement[s]; the two pairs of one expert hold equal values.
All inputs are finite; a program needn't handle non-finite values.
Results may differ from the reference program's by a relative error of at most 0.014.
Values may be sent and summed in bfloat16 or wider, within the bound.
No kernel may reach another device: no remote copies, remote signals or barrier semaphores. Data moves between devices by JAX's collectives and lax.ppermute only.
A program may use at most 128 MiB of HBM per device.

```python
import math
import jax
import jax.numpy as jnp
import numpy as np
from jax import lax

D = 4096
HEADS = 16
HEAD_DIM = 128
FFW = 7168
TOK_DEV = 128
REQ_SLOTS = 5
HALF = 64
EXPERTS = 4
CAP = 48
TOKENS = 2048
N_REQ = 16
N_TP = 2


def pair_experts(key):
    order = jax.random.permutation(jax.random.fold_in(key, 11), N_REQ // 2)
    return (order % EXPERTS).astype(jnp.int32)


def draw_placement(key, part):
    return pair_experts(key)


def device_owner(key):
    return jnp.repeat(pair_experts(key), 2)


def draw_w_gate_up(key, part):
    owner = device_owner(key)
    side = jnp.arange(N_REQ, dtype=jnp.int32) % 2

    def one_device(pair_info):
        expert = pair_info[0]
        half_index = pair_info[1]
        sub_key = jax.random.fold_in(jax.random.fold_in(key, 101 + expert), half_index)
        values = jax.random.truncated_normal(sub_key, -4.0, 4.0, (2, D, FFW // 2), jnp.float32)
        return (values * D ** (-0.5)).astype(jnp.bfloat16)
    return lax.map(one_device, jnp.stack([owner, side], axis=1))


def draw_w_down(key, part):
    owner = device_owner(key)
    side = jnp.arange(N_REQ, dtype=jnp.int32) % 2

    def one_device(pair_info):
        expert = pair_info[0]
        half_index = pair_info[1]
        sub_key = jax.random.fold_in(jax.random.fold_in(key, 301 + expert), half_index)
        values = jax.random.truncated_normal(sub_key, -4.0, 4.0, (FFW // 2, D), jnp.float32)
        return (values * FFW ** (-0.5)).astype(jnp.bfloat16)
    return lax.map(one_device, jnp.stack([owner, side], axis=1))


def draw_residual_in(key, part):
    own_key = jax.random.fold_in(key, 5)
    base_key, row_key, col_key = jax.random.split(own_key, 3)
    column = jnp.arange(D, dtype=jnp.float32) / D
    col_scale = 0.5 * 3.0 ** column * jax.random.uniform(col_key, (D,), jnp.float32, 0.7, 1.4)
    row_scale = 10.0 ** jax.random.uniform(row_key, (TOKENS, 1), jnp.float32, -0.5, 0.5)
    base = jax.random.truncated_normal(base_key, -6.0, 6.0, (TOKENS, D), jnp.float32)
    return (base * row_scale * col_scale).astype(jnp.bfloat16)


def level_of(key, shape, shards, low, largest):
    loudness, own = 1.0, jax.random.fold_in(key, 6)
    for position, shards_of in shards:
        draws = jnp.exp(jax.random.uniform(jax.random.fold_in(own, position), (shards_of,), jnp.float32, low / len(shards), largest / len(shards)))
        loudness = loudness * jnp.repeat(draws, shape[position] // shards_of).reshape([-1 if axis == position else 1 for axis in range(len(shape))])
    return loudness


def split_up(amount, total, reach, slope):
    portions = [(1 << 20) // math.isqrt(rank ** slope) + 1 for rank in range(2, amount + 1)]
    spare, counts = total - reach - (amount - 1), [1] * (amount - 1)
    while spare > 0:
        free = [i for i in range(amount - 1) if counts[i] < reach]
        pool, budget = sum([portions[i] for i in free]), spare
        for i in free:
            extra = min(reach - counts[i], max(1, budget * portions[i] // pool), spare)
            counts[i] = counts[i] + extra
            spare = spare - extra
    return np.array([reach] + counts)


def uneven_parts(key, count, total, limit, lean):
    if count == 2:
        one = jax.random.randint(key, (), max(1, total - limit), min(limit, total - 1) + 1)
        return jnp.stack([one, total - one])
    sizes = jnp.asarray(split_up(count, total, limit, lean), jnp.int32)
    couples = (count - 1) // 2
    giver, sink = sizes[1:1 + 2 * couples:2], sizes[2:2 + 2 * couples:2]
    room = jnp.minimum(giver - 1, limit - sink)
    passed = jax.random.randint(jax.random.fold_in(key, 1), (couples,), 0, 1 << 20) % (room + 1)
    sizes = sizes.at[1:1 + 2 * couples:2].set(giver - passed).at[2:2 + 2 * couples:2].set(sink + passed)
    return sizes[jax.random.permutation(jax.random.fold_in(key, 2), count)]


def deal_out(key, own, number, rows, number_of, top, reach, lean):
    ranking = jax.random.permutation(key, number_of)
    heavy_load, ordinary = portions_of(number_of, rows * top, reach, lean, True), portions_of(number_of, rows * top, reach, lean, False)
    places = jnp.arange(number_of)

    def named(sizes, offset_by):
        used = int((sizes > 0).sum())
        fixed = max(1, used // 4)
        moved = fixed + (places - fixed + offset_by * (used - fixed)) % max(1, number_of - fixed)
        return jnp.zeros((number_of,), jnp.int32).at[ranking[jnp.where(places < fixed, places, moved)]].set(jnp.asarray(sizes, jnp.int32))

    sizes = jnp.where(number % 4 == 0, named(heavy_load, number // 4), named(ordinary, number - number // 4 - 1))
    mixed = jax.random.permutation(jax.random.fold_in(own, 3), number_of)
    giver, taker = mixed[0:number_of // 2 * 2:2], mixed[1:number_of // 2 * 2:2]
    slack = jnp.minimum(sizes[giver] - 1, reach - sizes[taker]) // 2
    slack = jnp.where((giver == ranking[0]) | (taker == ranking[0]) | (sizes[taker] == 0), 0, jnp.maximum(slack, 0))
    moved = jax.random.randint(jax.random.fold_in(own, 4), (number_of // 2,), 0, 1 << 20) % (slack + 1)
    sizes = sizes.at[giver].add(-moved).at[taker].add(moved)
    labels = jnp.searchsorted(jnp.cumsum(sizes), jnp.arange(rows * top), side="right").astype(jnp.int32)
    grid = labels.reshape(top, rows).T
    grid = grid[jax.random.permutation(jax.random.fold_in(own, 1), rows)]
    offset_by = jax.random.randint(jax.random.fold_in(own, 2), (rows, 1), 0, top)
    return jnp.take_along_axis(grid, (jnp.arange(top)[None, :] + offset_by) % top, axis=1)


def portions_of(count, total, limit, skew, full):
    loads = [(1 << 20) // math.isqrt(grade ** skew) + 1 for grade in range(1, count + 1)]
    largest = limit if full else min(limit, max(-(-total // count), total * loads[0] // sum(loads)))
    least = 1 if total - largest >= count - 1 else 0
    counts, spare = [largest] + [least] * (count - 1), total - largest - least * (count - 1)
    while spare > 0:
        movable = [i for i in range(1, count) if counts[i] < largest] or [i for i in range(1, count) if counts[i] < limit]
        pool, left = sum([loads[i] for i in movable]), spare
        for i in movable:
            extra = min(limit - counts[i], max(1, left * loads[i] // pool), spare)
            counts[i] = counts[i] + extra
            spare = spare - extra
    return np.array(counts)


def gaussian(stream_key, extent, spread, reach, cuts=(), kind=jnp.bfloat16):
    result = spread * jax.random.normal(stream_key, extent, jnp.float32)
    if cuts:
        result = result * level_of(stream_key, extent, cuts, -0.22, 0.18)
    return jnp.clip(result, -reach, reach).astype(kind)


def setup_inputs(seed: int = 0) -> dict:
    arg_keys = jax.random.split(jax.random.key(seed), 12)
    attn_heads = gaussian(arg_keys[0], (TOKENS, HEADS * HEAD_DIM), 1.0, 6.0, ((0, 16), (1, 2)))
    residual_in = draw_residual_in(jax.random.fold_in(arg_keys[11], 71), 0)
    w_out = gaussian(arg_keys[2], (HEADS * HEAD_DIM, D), (HEADS * HEAD_DIM) ** -0.5, 0.125, ((0, 2),))
    gain_attn = jnp.clip(1.0 + 0.18 * jax.random.normal(arg_keys[3], (D,), jnp.float32), 0.1, 1.9)
    router = gaussian(arg_keys[4], (D, EXPERTS), D ** -0.5, 0.09375, ((0, 2),))
    expert_ids_keys = jax.random.split(jax.random.fold_in(arg_keys[5], 1), TOKENS // HALF)
    expert_ids_turns = jax.random.permutation(jax.random.fold_in(arg_keys[5], 3), TOKENS // HALF)
    expert_ids = jax.vmap(lambda own, number: deal_out(jax.random.fold_in(arg_keys[5], 2), own, number, HALF, EXPERTS, 2, CAP, 2))(expert_ids_keys, expert_ids_turns).reshape((TOKENS, 2))
    lengths = jax.vmap(lambda own: uneven_parts(own, REQ_SLOTS, TOK_DEV, HALF, 2))(jax.random.split(arg_keys[6], N_REQ)).reshape((N_REQ, REQ_SLOTS)).astype(jnp.int32)
    placement = draw_placement(jax.random.fold_in(arg_keys[11], 71), 0)
    w_gate_up = draw_w_gate_up(jax.random.fold_in(arg_keys[11], 71), 0)
    w_down = draw_w_down(jax.random.fold_in(arg_keys[11], 71), 0)
    gain_final = jnp.clip(1.0 + 0.18 * jax.random.normal(arg_keys[10], (D,), jnp.float32), 0.1, 1.9)
    return {"attn_heads": attn_heads, "residual_in": residual_in, "w_out": w_out, "gain_attn": gain_attn, "router": router, "expert_ids": expert_ids, "lengths": lengths, "placement": placement, "w_gate_up": w_gate_up, "w_down": w_down, "gain_final": gain_final}


epsilon = 1e-05

def inverse_rms(values):
    return lax.rsqrt(lax.optimization_barrier(jnp.mean(values * values, axis=-1, keepdims=True)) + epsilon)

def reference(attn_heads, residual_in, w_out, gain_attn, router, expert_ids, lengths, placement, w_gate_up, w_down, gain_final):
    state = residual_in.astype(jnp.float32) + jnp.dot(attn_heads, w_out, preferred_element_type=jnp.float32)
    normed = state * inverse_rms(state) * gain_attn
    normed_bf = normed.astype(jnp.bfloat16)
    logits = jnp.dot(normed, router.astype(jnp.float32), precision=lax.Precision.HIGHEST)
    chosen = jnp.take_along_axis(logits, expert_ids, axis=1)
    weights = jax.nn.sigmoid(chosen - chosen[:, ::-1])
    row_index = jnp.arange(TOKENS, dtype=jnp.int32)
    positions = row_index % TOK_DEV
    owners = row_index // TOK_DEV
    live_count = TOK_DEV - lengths[:, REQ_SLOTS - 1]
    live_rows = positions < live_count[owners]
    flat_ids = expert_ids.reshape(-1)
    flat_live = jnp.repeat(live_rows, 2)
    most_rows = 2 * N_REQ * CAP
    blocks = 2 * N_TP
    block_units = FFW // blocks

    def one_expert(expert, totals):
        first_pair = jnp.argmax(placement == expert).astype(jnp.int32)
        left_device = 2 * first_pair
        gate_left = lax.dynamic_index_in_dim(w_gate_up, left_device, 0, keepdims=False)
        gate_right = lax.dynamic_index_in_dim(w_gate_up, left_device + 1, 0, keepdims=False)
        gate_full = jnp.concatenate([gate_left, gate_right], axis=2)
        down_left = lax.dynamic_index_in_dim(w_down, left_device, 0, keepdims=False)
        down_right = lax.dynamic_index_in_dim(w_down, left_device + 1, 0, keepdims=False)
        down_full = jnp.concatenate([down_left, down_right], axis=0)
        selected = jnp.logical_and(flat_ids == expert, flat_live)
        picked_rows = jnp.nonzero(selected, size=most_rows, fill_value=0)[0].astype(jnp.int32)
        valid_rows = jnp.arange(most_rows) < jnp.sum(selected.astype(jnp.int32))
        rows_in = normed_bf[picked_rows // 2]
        gate_proj = jnp.dot(rows_in, gate_full[0], preferred_element_type=jnp.float32)
        up_proj = jnp.dot(rows_in, gate_full[1], preferred_element_type=jnp.float32)
        activ = (jax.nn.silu(gate_proj) * up_proj).astype(jnp.bfloat16)
        summed = jnp.zeros((most_rows, D), jnp.float32)
        for block in range(blocks):
            lower = block * block_units
            part_sum = jnp.dot(activ[:, lower:lower + block_units], down_full[lower:lower + block_units], preferred_element_type=jnp.float32)
            rounded = lax.optimization_barrier(part_sum.astype(jnp.bfloat16))
            summed = summed + rounded.astype(jnp.float32)
        summed = summed * valid_rows[:, None].astype(jnp.float32)
        return totals.at[picked_rows].add(summed)
    totals = lax.fori_loop(0, EXPERTS, one_expert, jnp.zeros((2 * TOKENS, D), jnp.float32))
    per_choice = totals.reshape(TOKENS, 2, D)
    mixture = per_choice[:, 0] * weights[:, 0:1] + per_choice[:, 1] * weights[:, 1:2]
    combined = state + mixture
    final_norm = combined * inverse_rms(combined) * gain_final
    return (combined.astype(jnp.bfloat16), final_norm.astype(jnp.bfloat16))
```

```python
import jax
import jax.numpy as jnp
from jax import lax
from jax.sharding import PartitionSpec as P

epsilon = 1e-05


def pair_shift(value, k, devices):
    return lax.ppermute(value, "req", [(i, 2 * ((i // 2) ^ k) + i % 2) for i in range(devices)])


def side_swap(value, devices):
    return lax.ppermute(value, "req", [(i, i ^ 1) for i in range(devices)])


def core_swap(value):
    return lax.ppermute(value, "tp", [(0, 1), (1, 0)])


def core_sum(value):
    if lax.axis_size("tp") == 2:
        return value + core_swap(value)
    return lax.psum(value, "tp")


def core_gather(value):
    if lax.axis_size("tp") != 2:
        return lax.all_gather(value, "tp", axis=1, tiled=True)
    other = core_swap(value)
    first = lax.axis_index("tp") == 0
    return jnp.concatenate([jnp.where(first, value, other), jnp.where(first, other, value)], axis=1)


def core_scatter(value):
    if lax.axis_size("tp") != 2:
        return lax.psum_scatter(
            value.astype(jnp.bfloat16), "tp", scatter_dimension=1, tiled=True
        ).astype(jnp.float32)
    width = value.shape[1] // 2
    first = lax.axis_index("tp") == 0
    low, high = value[:, :width], value[:, width:]
    away = jnp.where(first, high, low).astype(jnp.bfloat16)
    return jnp.where(first, low, high) + core_swap(away).astype(jnp.float32)


def on_device(
    attn_heads,
    residual_in,
    w_out,
    gain_attn,
    router,
    expert_ids,
    lengths,
    placement,
    w_gate_up,
    w_down,
    gain_final,
):
    tok_rows = attn_heads.shape[0]
    half_rows = tok_rows // 2
    feat_width = residual_in.shape[1]
    full_width = feat_width * lax.axis_size("tp")
    devices = lax.axis_size("req")
    pair_count = devices // 2
    expert_count = devices // 4
    capacity = min(half_rows, 3 * tok_rows // (2 * expert_count))
    own_pair = lax.axis_index("req") // 2

    expert_range = jnp.arange(expert_count, dtype=jnp.int32)
    row_index = jnp.arange(tok_rows, dtype=jnp.int32)
    live_rows = row_index < tok_rows - lengths[0, lengths.shape[1] - 1]
    held_table = (placement[:, None] == expert_range).astype(jnp.int32)
    pair_range = jnp.arange(pair_count, dtype=jnp.int32)[:, None]
    first_pair = jnp.min(jnp.where(held_table > 0, pair_range, pair_count), axis=0)
    second_pair = jnp.max(jnp.where(held_table > 0, pair_range, -1), axis=0)
    upper_half = (row_index >= half_rows)[:, None, None]
    block_table = jnp.where(upper_half, second_pair ^ own_pair, first_pair ^ own_pair)
    match_table = expert_ids[:, :, None] == expert_range
    id_hot = match_table & live_rows[:, None, None]
    named = jnp.sum(id_hot.astype(jnp.float32), axis=1)
    before = (row_index[:, None] > row_index[None, :]) & (
        (row_index[:, None] >= half_rows) == (row_index[None, :] >= half_rows)
    )
    running = jnp.dot(
        before.astype(jnp.bfloat16), named.astype(jnp.bfloat16), preferred_element_type=jnp.float32
    ).astype(jnp.int32)
    slot_index = jnp.sum(
        jnp.where(id_hot, block_table * capacity + running[:, None, :], 0), axis=2
    )
    slot_index = jnp.where(live_rows[:, None], slot_index, pair_count * capacity)
    slot_range = jnp.arange(pair_count * capacity, dtype=jnp.int32)
    place_hot = (
        (slot_index[:, 0][None, :] == slot_range[:, None])
        | (slot_index[:, 1][None, :] == slot_range[:, None])
    ).astype(jnp.bfloat16)

    partial_out = jnp.dot(attn_heads, w_out, preferred_element_type=jnp.float32)
    state = residual_in.astype(jnp.float32) + core_scatter(partial_out)
    square_sum = core_sum(jnp.sum(state * state, axis=1, keepdims=True))
    inverse = lax.rsqrt(square_sum / full_width + epsilon)
    scaled = state * gain_attn
    normed_bf = (scaled * inverse).astype(jnp.bfloat16)

    outgoing = jnp.dot(place_hot, normed_bf, preferred_element_type=jnp.float32).astype(jnp.bfloat16)
    outgoing = outgoing.reshape(pair_count, capacity, feat_width)
    chunks = [[k for k in range(pair_count) if (k // 2) % 2 == c] for c in range(2)]
    arrived = {}
    for chunk in chunks:
        for k in chunk:
            arrived[k] = pair_shift(outgoing[k], k, devices) if k else outgoing[k]

    logits = inverse * core_sum(
        jnp.dot(scaled, router.astype(jnp.float32), precision=lax.Precision.HIGHEST)
    )
    chosen = jnp.sum(match_table.astype(jnp.float32) * logits[:, None, :], axis=2)
    weights = jax.nn.sigmoid(chosen - chosen[:, ::-1])
    mix = jnp.where(slot_index[:, 0:1] == slot_range, weights[:, 0:1], 0.0) + jnp.where(
        slot_index[:, 1:2] == slot_range, weights[:, 1:2], 0.0
    )
    mix_high = lax.reduce_precision(mix, 8, 7)
    mix_low = (mix - mix_high).astype(jnp.bfloat16)
    mix_high = mix_high.astype(jnp.bfloat16)

    mixture = jnp.zeros_like(state)
    for chunk in chunks:
        groups = [chunk[i : i + 2] for i in range(0, len(chunk), 2)]
        mine = [jnp.concatenate([arrived[k] for k in group], axis=0) for group in groups]
        others = [side_swap(value, devices) for value in mine]
        rows = jnp.concatenate([core_gather(value) for value in mine + others], axis=0)
        gate_proj = jnp.dot(rows, w_gate_up[0, 0], preferred_element_type=jnp.float32)
        up_proj = jnp.dot(rows, w_gate_up[0, 1], preferred_element_type=jnp.float32)
        activ = (jax.nn.silu(gate_proj) * up_proj).astype(jnp.bfloat16)
        down_part = jnp.dot(activ, w_down[0], preferred_element_type=jnp.float32)
        reduced = core_scatter(down_part)
        near = len(chunk) * capacity
        away = reduced[near:].astype(jnp.bfloat16)
        step = 2 * capacity
        back = {}
        for g in reversed(range(len(groups))):
            swapped = side_swap(away[g * step : (g + 1) * step], devices).astype(jnp.float32)
            total = (reduced[g * step : (g + 1) * step] + swapped).astype(jnp.bfloat16)
            for j, k in enumerate(groups[g]):
                block = total[j * capacity : (j + 1) * capacity]
                back[k] = pair_shift(block, k, devices) if k else block
        returned = jnp.concatenate([back[k] for k in chunk], axis=0)
        pick = lambda table: jnp.concatenate(
            [table[:, k * capacity : (k + 1) * capacity] for k in chunk], axis=1
        )
        mixture += jnp.dot(pick(mix_high), returned, preferred_element_type=jnp.float32)
        mixture += jnp.dot(pick(mix_low), returned, preferred_element_type=jnp.float32)

    combined = state + mixture
    final_sum = core_sum(jnp.sum(combined * combined, axis=1, keepdims=True))
    final_scale = lax.rsqrt(final_sum / full_width + epsilon)
    return (
        combined.astype(jnp.bfloat16),
        (combined * final_scale * gain_final).astype(jnp.bfloat16),
    )


def solution(mesh):
    placed = (
        P("req", "tp"),
        P("req", "tp"),
        P("tp", None),
        P("tp"),
        P("tp", None),
        P("req", None),
        P("req", None),
        P(),
        P("req", None, None, "tp"),
        P("req", "tp", None),
        P("tp"),
    )
    return jax.shard_map(
        on_device,
        mesh=mesh,
        in_specs=placed,
        out_specs=(P("req", "tp"), P("req", "tp")),
        check_vma=False,
    )
```

```python
import jax
import jax.numpy as jnp
from jax import lax
from jax.experimental import pallas as pl
from jax.experimental.pallas import tpu as pltpu
from jax.sharding import PartitionSpec as P

epsilon = 1e-05
LONG = 20_000_000_000
WHOLE = pl.BlockSpec(memory_space=pltpu.VMEM)
ANYWHERE = pl.BlockSpec(memory_space=pl.ANY)


def pair_shift(value, k, devices):
    return lax.ppermute(value, "req", [(i, 2 * ((i // 2) ^ k) + i % 2) for i in range(devices)])


def side_swap(value, devices):
    return lax.ppermute(value, "req", [(i, i ^ 1) for i in range(devices)])


def core_swap(value):
    return lax.ppermute(value, "tp", [(0, 1), (1, 0)])


def core_sum(value):
    if lax.axis_size("tp") == 2:
        return value + core_swap(value)
    return lax.psum(value, "tp")


def core_gather(value):
    if lax.axis_size("tp") != 2:
        return lax.all_gather(value, "tp", axis=1, tiled=True)
    other = core_swap(value)
    first = lax.axis_index("tp") == 0
    return jnp.concatenate([jnp.where(first, value, other), jnp.where(first, other, value)], axis=1)


def core_scatter(value):
    if lax.axis_size("tp") != 2:
        return lax.psum_scatter(
            value.astype(jnp.bfloat16), "tp", scatter_dimension=1, tiled=True
        ).astype(jnp.float32)
    width = value.shape[1] // 2
    first = lax.axis_index("tp") == 0
    low, high = value[:, :width], value[:, width:]
    away = jnp.where(first, high, low).astype(jnp.bfloat16)
    return jnp.where(first, low, high) + core_swap(away).astype(jnp.float32)


def slot_rows_kernel(blocks, slots_ref, rows_ref, *refs):
    slots = slots_ref[...]
    for out_ref, block in zip(refs[-len(blocks) :], blocks):
        shape = (out_ref.shape[0], slots.shape[1])
        here = lax.broadcasted_iota(jnp.int32, shape, 0) + block * shape[0]
        hot = jnp.where((slots[0:1] == here) | (slots[1:2] == here), 1.0, 0.0)
        out_ref[...] = jnp.dot(
            hot.astype(jnp.bfloat16), rows_ref[...], preferred_element_type=jnp.float32
        ).astype(jnp.bfloat16)


def slot_rows(blocks, capacity, slots, rows, after):
    outs = pl.pallas_call(
        lambda *refs: slot_rows_kernel(blocks, *refs),
        in_specs=[WHOLE, WHOLE] + [ANYWHERE] * len(after),
        out_specs=[WHOLE] * len(blocks),
        out_shape=[jax.ShapeDtypeStruct((capacity, rows.shape[1]), jnp.bfloat16)] * len(blocks),
        compiler_params=pltpu.CompilerParams(vmem_limit_bytes=16 << 20),
        name="slot_rows",
    )(slots, rows, *after)
    return dict(zip(blocks, outs))


def join_kernel(count, *refs):
    out_ref = refs[-1]
    start = 0
    for ref in refs[:count]:
        out_ref[start : start + ref.shape[0]] = ref[...]
        start += ref.shape[0]


def join(values, after, flops=0):
    rows = sum(value.shape[0] for value in values)
    return pl.pallas_call(
        lambda *refs: join_kernel(len(values), *refs),
        in_specs=[WHOLE] * len(values) + [ANYWHERE] * len(after),
        out_specs=WHOLE,
        out_shape=jax.ShapeDtypeStruct((rows, values[0].shape[1]), values[0].dtype),
        compiler_params=pltpu.CompilerParams(vmem_limit_bytes=16 << 20),
        cost_estimate=pl.CostEstimate(flops=flops, bytes_accessed=0, transcendentals=0),
        name="join",
    )(*values, *after)


def add_cores_kernel(counts, kept_ref, other_ref, *refs):
    outs = refs[-len(counts) - 1 :]
    start = outs[0].shape[0]
    outs[0][...] = kept_ref[:start] + other_ref[:start].astype(jnp.float32)
    for out_ref, count in zip(outs[1:], counts):
        part = slice(start, start + count)
        out_ref[...] = (kept_ref[part] + other_ref[part].astype(jnp.float32)).astype(jnp.bfloat16)
        start += count


def add_cores(kept, other, counts, after):
    rows, width = kept.shape
    return pl.pallas_call(
        lambda *refs: add_cores_kernel(counts, *refs),
        in_specs=[WHOLE, WHOLE] + [ANYWHERE] * len(after),
        out_specs=[WHOLE] * (len(counts) + 1),
        out_shape=[jax.ShapeDtypeStruct((rows - sum(counts), width), jnp.float32)]
        + [jax.ShapeDtypeStruct((count, width), jnp.bfloat16) for count in counts],
        compiler_params=pltpu.CompilerParams(vmem_limit_bytes=16 << 20),
        name="add_cores",
    )(kept, other, *after)


def add_sides_kernel(start, own_ref, other_ref, *refs):
    total = own_ref[start : start + other_ref.shape[0]] + other_ref[...].astype(jnp.float32)
    first = 0
    for out_ref in refs:
        out_ref[...] = total[first : first + out_ref.shape[0]].astype(jnp.bfloat16)
        first += out_ref.shape[0]


def add_sides(own, start, other, counts, after):
    return pl.pallas_call(
        lambda *refs: add_sides_kernel(start, *refs[:2], *refs[-len(counts) :]),
        in_specs=[WHOLE, WHOLE] + [ANYWHERE] * len(after),
        out_specs=[WHOLE] * len(counts),
        out_shape=[jax.ShapeDtypeStruct((n, own.shape[1]), jnp.bfloat16) for n in counts],
        compiler_params=pltpu.CompilerParams(vmem_limit_bytes=16 << 20),
        name="add_sides",
    )(own, other, *after)


def gate_up_kernel(counts, core_ref, *refs):
    pieces = refs[: 2 * len(counts)]
    weights_ref = refs[2 * len(counts)]
    out_ref, rows_ref = refs[-2:]
    width = pieces[0].shape[1]

    @pl.when(pl.program_id(0) == 0)
    def _():
        start = 0
        own = pl.multiple_of(core_ref[0] * width, width)
        other = pl.multiple_of((1 - core_ref[0]) * width, width)
        for i, count in enumerate(counts):
            rows_ref[start : start + count, pl.ds(own, width)] = pieces[2 * i][...]
            rows_ref[start : start + count, pl.ds(other, width)] = pieces[2 * i + 1][...]
            start += count

    rows = rows_ref[...]
    gate = jnp.dot(rows, weights_ref[0, 0], preferred_element_type=jnp.float32)
    up = jnp.dot(rows, weights_ref[0, 1], preferred_element_type=jnp.float32)
    out_ref[...] = (gate * jax.nn.sigmoid(gate) * up).astype(jnp.bfloat16)


def gate_up(core, pieces, weights, after):
    counts = [own.shape[0] for own, _ in pieces]
    rows = sum(counts)
    _, _, depth, units = weights.shape
    block = 256
    return pl.pallas_call(
        lambda *refs: gate_up_kernel(counts, *refs),
        grid_spec=pltpu.PrefetchScalarGridSpec(
            num_scalar_prefetch=1,
            grid=(units // block,),
            in_specs=[WHOLE] * (2 * len(counts))
            + [pl.BlockSpec((1, 2, depth, block), lambda i, core: (0, 0, 0, i))]
            + [ANYWHERE] * len(after),
            out_specs=pl.BlockSpec((rows, block), lambda i, core: (0, i)),
            scratch_shapes=[pltpu.VMEM((rows, depth), jnp.bfloat16)],
        ),
        out_shape=jax.ShapeDtypeStruct((rows, units), jnp.bfloat16),
        compiler_params=pltpu.CompilerParams(vmem_limit_bytes=36 << 20),
        cost_estimate=pl.CostEstimate(
            flops=rows * depth, bytes_accessed=depth, transcendentals=0
        ),
        name="gate_up",
    )(core, *[part for piece in pieces for part in piece], weights, *after)


def down_kernel(core_ref, activ_ref, weights_ref, *refs):
    out_ref = refs[-1]
    out_ref[...] = jnp.dot(
        activ_ref[...], weights_ref[0], preferred_element_type=jnp.float32
    ).astype(out_ref.dtype)


def down(core, activ, weights, away, after):
    rows, units = activ.shape
    width = weights.shape[2] // 2
    block = 1024
    steps = width // block
    return pl.pallas_call(
        down_kernel,
        grid_spec=pltpu.PrefetchScalarGridSpec(
            num_scalar_prefetch=1,
            grid=(steps,),
            in_specs=[
                pl.BlockSpec((rows, units), lambda i, core: (0, 0)),
                pl.BlockSpec(
                    (1, units, block),
                    lambda i, core: (0, 0, (1 - core[0] if away else core[0]) * steps + i),
                ),
            ]
            + [ANYWHERE] * len(after),
            out_specs=pl.BlockSpec((rows, block), lambda i, core: (0, i)),
        ),
        out_shape=jax.ShapeDtypeStruct((rows, width), jnp.bfloat16 if away else jnp.float32),
        compiler_params=pltpu.CompilerParams(vmem_limit_bytes=44 << 20),
        cost_estimate=pl.CostEstimate(
            flops=rows * units, bytes_accessed=units, transcendentals=0
        ),
        name="down_away" if away else "down_own",
    )(core, activ, weights, *after)


def down_both_kernel(core_ref, activ_ref, weights_ref, *refs):
    away_ref, own_ref = refs[-2:]
    product = jnp.dot(activ_ref[...], weights_ref[0], preferred_element_type=jnp.float32)
    half = pl.num_programs(0) // 2

    @pl.when(pl.program_id(0) < half)
    def _():
        away_ref[...] = product.astype(jnp.bfloat16)

    @pl.when(pl.program_id(0) >= half)
    def _():
        own_ref[...] = product


def down_both(core, activ, weights, after):
    rows, units = activ.shape
    width = weights.shape[2] // 2
    block = 1024
    half = width // block

    def columns(i, core):
        side = jnp.where(i < half, 1 - core[0], core[0])
        return (0, 0, side * half + lax.rem(i, half))

    return pl.pallas_call(
        down_both_kernel,
        grid_spec=pltpu.PrefetchScalarGridSpec(
            num_scalar_prefetch=1,
            grid=(2 * half,),
            in_specs=[
                pl.BlockSpec((rows, units), lambda i, core: (0, 0)),
                pl.BlockSpec((1, units, block), columns),
            ]
            + [ANYWHERE] * len(after),
            out_specs=[
                pl.BlockSpec((rows, block), lambda i, core: (0, jnp.minimum(i, half - 1))),
                pl.BlockSpec((rows, block), lambda i, core: (0, jnp.maximum(i - half, 0))),
            ],
        ),
        out_shape=[
            jax.ShapeDtypeStruct((rows, width), jnp.bfloat16),
            jax.ShapeDtypeStruct((rows, width), jnp.float32),
        ],
        compiler_params=pltpu.CompilerParams(vmem_limit_bytes=44 << 20),
        cost_estimate=pl.CostEstimate(flops=rows * units, bytes_accessed=units, transcendentals=0),
        name="down_both",
    )(core, activ, weights, *after)


def mix_kernel(count, high_ref, low_ref, base_ref, *refs):
    out_ref = refs[-1]
    total = base_ref[...]
    width = high_ref.shape[1] // count
    for j, ref in enumerate(refs[:count]):
        part = slice(j * width, (j + 1) * width)
        total += jnp.dot(high_ref[:, part], ref[...], preferred_element_type=jnp.float32)
        total += jnp.dot(low_ref[:, part], ref[...], preferred_element_type=jnp.float32)
    out_ref[...] = total


def mix(tables, base, values, after, flops=0):
    return pl.pallas_call(
        lambda *refs: mix_kernel(len(values), *refs),
        in_specs=[WHOLE] * (3 + len(values)) + [ANYWHERE] * len(after),
        out_specs=WHOLE,
        out_shape=jax.ShapeDtypeStruct(base.shape, jnp.float32),
        compiler_params=pltpu.CompilerParams(vmem_limit_bytes=16 << 20),
        cost_estimate=pl.CostEstimate(flops=flops, bytes_accessed=0, transcendentals=0),
        name="mix",
    )(*tables, base, *values, *after)


def experts_of_two_cores(slots, rows, capacity, tables, state, w_gate_up, w_down, devices):
    pair_count = devices // 2
    core = lax.axis_index("tp").reshape(1)
    blocks = list(range(pair_count))
    quarter = pair_count // 4
    near, near_later, far, far_later = [
        blocks[i * quarter : (i + 1) * quarter] for i in range(4)
    ]
    size = quarter * capacity

    def columns(first):
        return [table[:, first * capacity : (first + quarter) * capacity] for table in tables]

    def send(group, values):
        return [pair_shift(x, k, devices) if k else x for k, x in zip(group, values)]

    outgoing = slot_rows(far + near + near_later, capacity, slots, rows, [])
    arrived = dict(zip(far, send(far, [outgoing[k] for k in far])))
    arrived |= zip(near, send(near, [outgoing[k] for k in near]))
    arrived |= zip(near_later, send(near_later, [outgoing[k] for k in near_later]))
    outgoing = slot_rows(far_later, capacity, slots, rows, [arrived[near[-1]]])
    arrived |= zip(far_later, send(far_later, [outgoing[k] for k in far_later]))

    near_own = join([arrived[k] for k in near], [])
    near_nbr = side_swap(near_own, devices)
    far_own = join([arrived[k] for k in far], [], LONG)
    far_nbr = side_swap(far_own, devices)
    near_later_own = join([arrived[k] for k in near_later], [])
    near_later_nbr = side_swap(near_later_own, devices)
    far_later_own = join([arrived[k] for k in far_later], [], LONG)
    far_later_nbr = side_swap(far_later_own, devices)

    pieces = [(x, core_swap(x)) for x in (far_own, near_own, far_nbr, near_nbr)]
    activ = gate_up(core, pieces, w_gate_up, [near_later_own, far_later_own])
    later = join([far_later_nbr, near_later_nbr], [activ])
    away = core_swap(down(core, activ, w_down, True, [later]))
    kept = down(core, activ, w_down, False, [])
    own, far_other, near_other = add_cores(kept, away, [size, size], [])
    pieces = [(x, core_swap(x)) for x in (far_later_own, near_later_own, later)]
    activ = gate_up(core, pieces, w_gate_up, [own])

    far_other = side_swap(far_other, devices)
    near_other = side_swap(near_other, devices)
    far_back = send(far, add_sides(own, 0, far_other, [capacity] * quarter, [activ]))
    totals = add_sides(own, size, near_other, [capacity] * quarter, [activ])
    near_back = send(near, totals)
    away, kept = down_both(core, activ, w_down, totals)
    state = mix(columns(far[0]), state, far_back, [kept], LONG)
    state = mix(columns(near[0]), state, near_back, [])
    counts = [capacity] * quarter + [size]
    own, *others = add_cores(kept, core_swap(away), counts, [state])
    far_back = []
    for j, k in enumerate(far_later):
        other = side_swap(others[j], devices)
        (total,) = add_sides(own, j * capacity, other, [capacity], [])
        far_back += send([k], [total])
    other = side_swap(others[-1], devices)
    near_back = send(near_later, add_sides(own, size, other, [capacity] * quarter, []))
    state = mix(columns(near_later[0]), state, near_back, [])
    return mix(columns(far_later[0]), state, far_back, [])


def experts_of_any(slots, rows, capacity, tables, state, w_gate_up, w_down, devices):
    pair_count = devices // 2
    slot_range = jnp.arange(pair_count * capacity, dtype=jnp.int32)[:, None]
    hot = ((slots[0:1] == slot_range) | (slots[1:2] == slot_range)).astype(jnp.bfloat16)
    outgoing = jnp.dot(hot, rows, preferred_element_type=jnp.float32).astype(jnp.bfloat16)
    outgoing = outgoing.reshape(pair_count, capacity, -1)
    own = [pair_shift(outgoing[k], k, devices) if k else outgoing[k] for k in range(pair_count)]
    own = jnp.concatenate(own, axis=0)
    rows = core_gather(jnp.concatenate([own, side_swap(own, devices)], axis=0))
    gate_proj = jnp.dot(rows, w_gate_up[0, 0], preferred_element_type=jnp.float32)
    up_proj = jnp.dot(rows, w_gate_up[0, 1], preferred_element_type=jnp.float32)
    activ = (jax.nn.silu(gate_proj) * up_proj).astype(jnp.bfloat16)
    reduced = core_scatter(jnp.dot(activ, w_down[0], preferred_element_type=jnp.float32))
    half = own.shape[0]
    swapped = side_swap(reduced[half:].astype(jnp.bfloat16), devices)
    total = (reduced[:half] + swapped.astype(jnp.float32)).astype(jnp.bfloat16)
    total = total.reshape(pair_count, capacity, -1)
    back = [pair_shift(total[k], k, devices) if k else total[k] for k in range(pair_count)]
    back = jnp.concatenate(back, axis=0)
    for table in tables:
        state += jnp.dot(table, back, preferred_element_type=jnp.float32)
    return state


def on_device(
    attn_heads,
    residual_in,
    w_out,
    gain_attn,
    router,
    expert_ids,
    lengths,
    placement,
    w_gate_up,
    w_down,
    gain_final,
):
    tok_rows = attn_heads.shape[0]
    half_rows = tok_rows // 2
    feat_width = residual_in.shape[1]
    full_width = feat_width * lax.axis_size("tp")
    devices = lax.axis_size("req")
    pair_count = devices // 2
    expert_count = devices // 4
    capacity = min(half_rows, 3 * tok_rows // (2 * expert_count))
    own_pair = lax.axis_index("req") // 2

    expert_range = jnp.arange(expert_count, dtype=jnp.int32)
    row_index = jnp.arange(tok_rows, dtype=jnp.int32)
    live_rows = row_index < tok_rows - lengths[0, lengths.shape[1] - 1]
    held_table = (placement[:, None] == expert_range).astype(jnp.int32)
    pair_range = jnp.arange(pair_count, dtype=jnp.int32)[:, None]
    first_pair = jnp.min(jnp.where(held_table > 0, pair_range, pair_count), axis=0)
    second_pair = jnp.max(jnp.where(held_table > 0, pair_range, -1), axis=0)
    upper_half = (row_index >= half_rows)[:, None, None]
    dest_table = jnp.where(upper_half, second_pair, first_pair)
    block_table = dest_table ^ own_pair
    match_table = expert_ids[:, :, None] == expert_range
    id_hot = match_table & live_rows[:, None, None]
    named = jnp.sum(id_hot.astype(jnp.float32), axis=1)
    before = (row_index[:, None] > row_index[None, :]) & (
        (row_index[:, None] >= half_rows) == (row_index[None, :] >= half_rows)
    )
    running = jnp.dot(
        before.astype(jnp.bfloat16), named.astype(jnp.bfloat16), preferred_element_type=jnp.float32
    ).astype(jnp.int32)
    slot_index = jnp.sum(
        jnp.where(id_hot, block_table * capacity + running[:, None, :], 0), axis=2
    )
    slot_index = jnp.where(live_rows[:, None], slot_index, pair_count * capacity)
    slot_range = jnp.arange(pair_count * capacity, dtype=jnp.int32)

    partial_out = jnp.dot(attn_heads, w_out, preferred_element_type=jnp.float32)
    state = residual_in.astype(jnp.float32) + core_scatter(partial_out)
    square_sum = core_sum(jnp.sum(state * state, axis=1, keepdims=True))
    inverse = lax.rsqrt(square_sum / full_width + epsilon)
    scaled = state * gain_attn
    normed_bf = (scaled * inverse).astype(jnp.bfloat16)

    logits = inverse * core_sum(
        jnp.dot(scaled, router.astype(jnp.float32), precision=lax.Precision.HIGHEST)
    )
    chosen = jnp.sum(match_table.astype(jnp.float32) * logits[:, None, :], axis=2)
    weights = jax.nn.sigmoid(chosen - chosen[:, ::-1])
    mix = jnp.where(slot_index[:, 0:1] == slot_range, weights[:, 0:1], 0.0) + jnp.where(
        slot_index[:, 1:2] == slot_range, weights[:, 1:2], 0.0
    )
    mix_high = lax.reduce_precision(mix, 8, 7)
    mix_low = (mix - mix_high).astype(jnp.bfloat16)
    mix_high = mix_high.astype(jnp.bfloat16)

    run = experts_of_two_cores if lax.axis_size("tp") == 2 else experts_of_any
    tables = (mix_high, mix_low)
    combined = run(slot_index.T, normed_bf, capacity, tables, state, w_gate_up, w_down, devices)
    final_sum = core_sum(jnp.sum(combined * combined, axis=1, keepdims=True))
    final_scale = lax.rsqrt(final_sum / full_width + epsilon)
    return (
        combined.astype(jnp.bfloat16),
        (combined * final_scale * gain_final).astype(jnp.bfloat16),
    )


def solution(mesh):
    placed = (
        P("req", "tp"),
        P("req", "tp"),
        P("tp", None),
        P("tp"),
        P("tp", None),
        P("req", None),
        P("req", None),
        P(),
        P("req", None, None, "tp"),
        P("req", "tp", None),
        P("tp"),
    )
    return jax.shard_map(
        on_device,
        mesh=mesh,
        in_specs=placed,
        out_specs=(P("req", "tp"), P("req", "tp")),
        check_vma=False,
    )
```

```python
import jax
import jax.numpy as jnp
from jax import lax
from jax.experimental import pallas as pl
from jax.experimental.pallas import tpu as pltpu
from jax.sharding import PartitionSpec as P

epsilon = 1e-05
UNITS = 256
LONG = 20_000_000_000
WHOLE = pl.BlockSpec(memory_space=pltpu.VMEM)
ANYWHERE = pl.BlockSpec(memory_space=pl.ANY)


def pair_shift(value, k, devices):
    return lax.ppermute(value, "req", [(i, 2 * ((i // 2) ^ k) + i % 2) for i in range(devices)])


def side_swap(value, devices):
    return lax.ppermute(value, "req", [(i, i ^ 1) for i in range(devices)])


def core_swap(value):
    return lax.ppermute(value, "tp", [(0, 1), (1, 0)])


def core_sum(value):
    if lax.axis_size("tp") == 2:
        return value + core_swap(value)
    return lax.psum(value, "tp")


def core_gather(value):
    if lax.axis_size("tp") != 2:
        return lax.all_gather(value, "tp", axis=1, tiled=True)
    other = core_swap(value)
    first = lax.axis_index("tp") == 0
    return jnp.concatenate([jnp.where(first, value, other), jnp.where(first, other, value)], axis=1)


def core_scatter(value):
    if lax.axis_size("tp") != 2:
        return lax.psum_scatter(
            value.astype(jnp.bfloat16), "tp", scatter_dimension=1, tiled=True
        ).astype(jnp.float32)
    width = value.shape[1] // 2
    first = lax.axis_index("tp") == 0
    low, high = value[:, :width], value[:, width:]
    away = jnp.where(first, high, low).astype(jnp.bfloat16)
    return jnp.where(first, low, high) + core_swap(away).astype(jnp.float32)


def slot_rows_kernel(blocks, slots_ref, rows_ref, *refs):
    slots = slots_ref[...]
    for out_ref, block in zip(refs[-len(blocks) :], blocks):
        shape = (out_ref.shape[0], slots.shape[1])
        here = lax.broadcasted_iota(jnp.int32, shape, 0) + block * shape[0]
        hot = jnp.where((slots[0:1] == here) | (slots[1:2] == here), 1.0, 0.0)
        out_ref[...] = jnp.dot(
            hot.astype(jnp.bfloat16), rows_ref[...], preferred_element_type=jnp.float32
        ).astype(jnp.bfloat16)


def slot_rows(blocks, capacity, slots, rows, after):
    outs = pl.pallas_call(
        lambda *refs: slot_rows_kernel(blocks, *refs),
        in_specs=[WHOLE, WHOLE] + [ANYWHERE] * len(after),
        out_specs=[WHOLE] * len(blocks),
        out_shape=[jax.ShapeDtypeStruct((capacity, rows.shape[1]), jnp.bfloat16)] * len(blocks),
        compiler_params=pltpu.CompilerParams(vmem_limit_bytes=16 << 20),
        name="slot_rows",
    )(slots, rows, *after)
    return dict(zip(blocks, outs))


def join_kernel(count, *refs):
    out_ref = refs[-1]
    start = 0
    for ref in refs[:count]:
        out_ref[start : start + ref.shape[0]] = ref[...]
        start += ref.shape[0]


def join(values, after, flops=0):
    rows = sum(value.shape[0] for value in values)
    return pl.pallas_call(
        lambda *refs: join_kernel(len(values), *refs),
        in_specs=[WHOLE] * len(values) + [ANYWHERE] * len(after),
        out_specs=WHOLE,
        out_shape=jax.ShapeDtypeStruct((rows, values[0].shape[1]), values[0].dtype),
        compiler_params=pltpu.CompilerParams(vmem_limit_bytes=16 << 20),
        cost_estimate=pl.CostEstimate(flops=flops, bytes_accessed=0, transcendentals=0),
        name="join",
    )(*values, *after)


def add_cores_kernel(counts, kept_ref, other_ref, *refs):
    outs = refs[-len(counts) - 1 :]
    start = outs[0].shape[0]
    outs[0][...] = kept_ref[:start] + other_ref[:start].astype(jnp.float32)
    for out_ref, count in zip(outs[1:], counts):
        part = slice(start, start + count)
        out_ref[...] = (kept_ref[part] + other_ref[part].astype(jnp.float32)).astype(jnp.bfloat16)
        start += count


def add_cores(kept, other, counts, after):
    rows, width = kept.shape
    return pl.pallas_call(
        lambda *refs: add_cores_kernel(counts, *refs),
        in_specs=[WHOLE, WHOLE] + [ANYWHERE] * len(after),
        out_specs=[WHOLE] * (len(counts) + 1),
        out_shape=[jax.ShapeDtypeStruct((rows - sum(counts), width), jnp.float32)]
        + [jax.ShapeDtypeStruct((count, width), jnp.bfloat16) for count in counts],
        compiler_params=pltpu.CompilerParams(vmem_limit_bytes=16 << 20),
        name="add_cores",
    )(kept, other, *after)


def add_sides_kernel(start, own_ref, other_ref, *refs):
    total = own_ref[start : start + other_ref.shape[0]] + other_ref[...].astype(jnp.float32)
    first = 0
    for out_ref in refs:
        out_ref[...] = total[first : first + out_ref.shape[0]].astype(jnp.bfloat16)
        first += out_ref.shape[0]


def add_sides(own, start, other, counts, after):
    return pl.pallas_call(
        lambda *refs: add_sides_kernel(start, *refs[:2], *refs[-len(counts) :]),
        in_specs=[WHOLE, WHOLE] + [ANYWHERE] * len(after),
        out_specs=[WHOLE] * len(counts),
        out_shape=[jax.ShapeDtypeStruct((n, own.shape[1]), jnp.bfloat16) for n in counts],
        compiler_params=pltpu.CompilerParams(vmem_limit_bytes=16 << 20),
        name="add_sides",
    )(own, other, *after)


def gate_up_kernel(counts, core_ref, *refs):
    pieces = refs[: 2 * len(counts)]
    weights_ref = refs[2 * len(counts)]
    out_ref, rows_ref = refs[-2:]
    width = pieces[0].shape[1]

    @pl.when(pl.program_id(0) == 0)
    def _():
        start = 0
        own = pl.multiple_of(core_ref[0] * width, width)
        other = pl.multiple_of((1 - core_ref[0]) * width, width)
        for i, count in enumerate(counts):
            rows_ref[start : start + count, pl.ds(own, width)] = pieces[2 * i][...]
            rows_ref[start : start + count, pl.ds(other, width)] = pieces[2 * i + 1][...]
            start += count

    rows = rows_ref[...]
    gate = jnp.dot(rows, weights_ref[0, 0], preferred_element_type=jnp.float32)
    up = jnp.dot(rows, weights_ref[0, 1], preferred_element_type=jnp.float32)
    out_ref[...] = (gate * jax.nn.sigmoid(gate) * up).astype(jnp.bfloat16)


def gate_up(core, pieces, weights, after, blocks=None):
    counts = [own.shape[0] for own, _ in pieces]
    rows = sum(counts)
    depth = weights.shape[2]
    block = UNITS
    first, last = blocks or (0, weights.shape[3] // block)
    units = (last - first) * block
    return pl.pallas_call(
        lambda *refs: gate_up_kernel(counts, *refs),
        grid_spec=pltpu.PrefetchScalarGridSpec(
            num_scalar_prefetch=1,
            grid=(units // block,),
            in_specs=[WHOLE] * (2 * len(counts))
            + [pl.BlockSpec((1, 2, depth, block), lambda i, core: (0, 0, 0, first + i))]
            + [ANYWHERE] * len(after),
            out_specs=pl.BlockSpec((rows, block), lambda i, core: (0, i)),
            scratch_shapes=[pltpu.VMEM((rows, depth), jnp.bfloat16)],
        ),
        out_shape=jax.ShapeDtypeStruct((rows, units), jnp.bfloat16),
        compiler_params=pltpu.CompilerParams(vmem_limit_bytes=36 << 20),
        cost_estimate=pl.CostEstimate(
            flops=rows * depth, bytes_accessed=depth, transcendentals=0
        ),
        name="gate_up",
    )(core, *[part for piece in pieces for part in piece], weights, *after)


def down_kernel(core_ref, activ_ref, weights_ref, *refs):
    out_ref = refs[-1]
    out_ref[...] = jnp.dot(
        activ_ref[...], weights_ref[0], preferred_element_type=jnp.float32
    ).astype(out_ref.dtype)


def down(core, activ, weights, away, after, flops=0):
    rows, units = activ.shape
    width = weights.shape[2] // 2
    block = 1024
    steps = width // block
    return pl.pallas_call(
        down_kernel,
        grid_spec=pltpu.PrefetchScalarGridSpec(
            num_scalar_prefetch=1,
            grid=(steps,),
            in_specs=[
                pl.BlockSpec((rows, units), lambda i, core: (0, 0)),
                pl.BlockSpec(
                    (1, units, block),
                    lambda i, core: (0, 0, (1 - core[0] if away else core[0]) * steps + i),
                ),
            ]
            + [ANYWHERE] * len(after),
            out_specs=pl.BlockSpec((rows, block), lambda i, core: (0, i)),
        ),
        out_shape=jax.ShapeDtypeStruct((rows, width), jnp.bfloat16 if away else jnp.float32),
        compiler_params=pltpu.CompilerParams(vmem_limit_bytes=44 << 20),
        cost_estimate=pl.CostEstimate(
            flops=flops or rows * units, bytes_accessed=units, transcendentals=0
        ),
        name="down_away" if away else "down_own",
    )(core, activ, weights, *after)


def down_both_kernel(count, core_ref, *refs):
    weights_ref = refs[count]
    away_ref, own_ref = refs[-2:]
    product, start = 0.0, 0
    for ref in refs[:count]:
        part = weights_ref[0, start : start + ref.shape[1]]
        product += jnp.dot(ref[...], part, preferred_element_type=jnp.float32)
        start += ref.shape[1]
    half = pl.num_programs(0) // 2

    @pl.when(pl.program_id(0) < half)
    def _():
        away_ref[...] = product.astype(jnp.bfloat16)

    @pl.when(pl.program_id(0) >= half)
    def _():
        own_ref[...] = product


def down_both(core, activ, weights, after):
    rows, units = activ[0].shape[0], weights.shape[1]
    width = weights.shape[2] // 2
    block = 1024
    half = width // block

    def columns(i, core):
        side = jnp.where(i < half, 1 - core[0], core[0])
        return (0, 0, side * half + lax.rem(i, half))

    return pl.pallas_call(
        lambda *refs: down_both_kernel(len(activ), *refs),
        grid_spec=pltpu.PrefetchScalarGridSpec(
            num_scalar_prefetch=1,
            grid=(2 * half,),
            in_specs=[
                pl.BlockSpec((rows, part.shape[1]), lambda i, core: (0, 0)) for part in activ
            ]
            + [pl.BlockSpec((1, units, block), columns)]
            + [ANYWHERE] * len(after),
            out_specs=[
                pl.BlockSpec((rows, block), lambda i, core: (0, jnp.minimum(i, half - 1))),
                pl.BlockSpec((rows, block), lambda i, core: (0, jnp.maximum(i - half, 0))),
            ],
        ),
        out_shape=[
            jax.ShapeDtypeStruct((rows, width), jnp.bfloat16),
            jax.ShapeDtypeStruct((rows, width), jnp.float32),
        ],
        compiler_params=pltpu.CompilerParams(vmem_limit_bytes=44 << 20),
        cost_estimate=pl.CostEstimate(flops=rows * units, bytes_accessed=units, transcendentals=0),
        name="down_both",
    )(core, *activ, weights, *after)


def mix_kernel(count, high_ref, low_ref, base_ref, *refs):
    out_ref = refs[-1]
    total = base_ref[...]
    width = high_ref.shape[1] // count
    for j, ref in enumerate(refs[:count]):
        part = slice(j * width, (j + 1) * width)
        total += jnp.dot(high_ref[:, part], ref[...], preferred_element_type=jnp.float32)
        total += jnp.dot(low_ref[:, part], ref[...], preferred_element_type=jnp.float32)
    out_ref[...] = total


def mix(tables, base, values, after, flops=0):
    return pl.pallas_call(
        lambda *refs: mix_kernel(len(values), *refs),
        in_specs=[WHOLE] * (3 + len(values)) + [ANYWHERE] * len(after),
        out_specs=WHOLE,
        out_shape=jax.ShapeDtypeStruct(base.shape, jnp.float32),
        compiler_params=pltpu.CompilerParams(vmem_limit_bytes=16 << 20),
        cost_estimate=pl.CostEstimate(flops=flops, bytes_accessed=0, transcendentals=0),
        name="mix",
    )(*tables, base, *values, *after)


def experts_of_two_cores(slots, rows, capacity, tables, state, w_gate_up, w_down, devices):
    pair_count = devices // 2
    core = lax.axis_index("tp").reshape(1)
    blocks = list(range(pair_count))
    quarter = pair_count // 4
    near, near_later, far, far_later = [
        blocks[i * quarter : (i + 1) * quarter] for i in range(4)
    ]
    size = quarter * capacity

    def columns(first):
        return [table[:, first * capacity : (first + quarter) * capacity] for table in tables]

    def send(group, values):
        return [pair_shift(x, k, devices) if k else x for k, x in zip(group, values)]

    outgoing = slot_rows(far + near + near_later, capacity, slots, rows, [])
    arrived = dict(zip(far, send(far, [outgoing[k] for k in far])))
    arrived |= zip(near, send(near, [outgoing[k] for k in near]))
    arrived |= zip(near_later, send(near_later, [outgoing[k] for k in near_later]))
    later = slot_rows(far_later, capacity, slots, rows, [arrived[near[-1]]])
    arrived |= zip(far_later, send(far_later, [later[k] for k in far_later]))

    spare = join([outgoing[near[0]]], [], LONG)
    near_own = join([arrived[k] for k in near], [])
    near_nbr = join([side_swap(near_own, devices)], [spare])
    far_own = join([arrived[k] for k in far], [near_nbr])
    far_nbr = side_swap(far_own, devices)
    near_later_own = join([arrived[k] for k in near_later], [near_nbr])
    near_later_nbr = side_swap(near_later_own, devices)

    pieces = [(x, core_swap(x)) for x in (far_own, near_own, far_nbr, near_nbr)]
    activ = gate_up(core, pieces, w_gate_up, [near_later_own])
    far_later_own = join([arrived[k] for k in far_later], [activ])
    far_later_nbr = side_swap(far_later_own, devices)
    near_later_nbr = join([near_later_nbr], [activ])
    away = down(core, activ, w_down, True, [far_later_own, near_later_nbr])
    far_later_nbr = join([far_later_nbr], [away])
    away = core_swap(away)
    kept = down(core, activ, w_down, False, [far_later_nbr], LONG)
    own, far_other, near_other = add_cores(kept, away, [size, size], [])
    pieces = [far_later_own, near_later_own, far_later_nbr, near_later_nbr]
    pieces = [(x, core_swap(x)) for x in pieces]
    unit_blocks = w_gate_up.shape[3] // UNITS
    split = unit_blocks // 2 + 1
    activ = [gate_up(core, pieces, w_gate_up, [own], (0, split))]

    far_other = side_swap(far_other, devices)
    near_other = side_swap(near_other, devices)
    totals = add_sides(own, 0, far_other, [capacity] * quarter, activ[:1])
    far_back = send(far, totals)
    activ.append(gate_up(core, pieces, w_gate_up, totals, (split, unit_blocks)))
    totals = add_sides(own, size, near_other, [capacity] * quarter, activ[1:])
    near_back = send(near, totals)
    away, kept = down_both(core, activ, w_down, totals)
    state = mix(columns(far[0]), state, far_back, [kept], LONG)
    state = mix(columns(near[0]), state, near_back, [])
    own, *others = add_cores(kept, core_swap(away), [capacity] * 2 * quarter, [state])
    back = []
    for j, k in enumerate(far_later + near_later):
        other = side_swap(others[j], devices)
        back += send([k], add_sides(own, j * capacity, other, [capacity], []))
    state = mix(columns(far_later[0]), state, back[:quarter], [], LONG)
    return mix(columns(near_later[0]), state, back[quarter:], [])


def experts_of_any(slots, rows, capacity, tables, state, w_gate_up, w_down, devices):
    pair_count = devices // 2
    slot_range = jnp.arange(pair_count * capacity, dtype=jnp.int32)[:, None]
    hot = ((slots[0:1] == slot_range) | (slots[1:2] == slot_range)).astype(jnp.bfloat16)
    outgoing = jnp.dot(hot, rows, preferred_element_type=jnp.float32).astype(jnp.bfloat16)
    outgoing = outgoing.reshape(pair_count, capacity, -1)
    own = [pair_shift(outgoing[k], k, devices) if k else outgoing[k] for k in range(pair_count)]
    own = jnp.concatenate(own, axis=0)
    rows = core_gather(jnp.concatenate([own, side_swap(own, devices)], axis=0))
    gate_proj = jnp.dot(rows, w_gate_up[0, 0], preferred_element_type=jnp.float32)
    up_proj = jnp.dot(rows, w_gate_up[0, 1], preferred_element_type=jnp.float32)
    activ = (jax.nn.silu(gate_proj) * up_proj).astype(jnp.bfloat16)
    reduced = core_scatter(jnp.dot(activ, w_down[0], preferred_element_type=jnp.float32))
    half = own.shape[0]
    swapped = side_swap(reduced[half:].astype(jnp.bfloat16), devices)
    total = (reduced[:half] + swapped.astype(jnp.float32)).astype(jnp.bfloat16)
    total = total.reshape(pair_count, capacity, -1)
    back = [pair_shift(total[k], k, devices) if k else total[k] for k in range(pair_count)]
    back = jnp.concatenate(back, axis=0)
    for table in tables:
        state += jnp.dot(table, back, preferred_element_type=jnp.float32)
    return state


def on_device(
    attn_heads,
    residual_in,
    w_out,
    gain_attn,
    router,
    expert_ids,
    lengths,
    placement,
    w_gate_up,
    w_down,
    gain_final,
):
    tok_rows = attn_heads.shape[0]
    half_rows = tok_rows // 2
    feat_width = residual_in.shape[1]
    full_width = feat_width * lax.axis_size("tp")
    devices = lax.axis_size("req")
    pair_count = devices // 2
    expert_count = devices // 4
    capacity = min(half_rows, 3 * tok_rows // (2 * expert_count))
    own_pair = lax.axis_index("req") // 2

    expert_range = jnp.arange(expert_count, dtype=jnp.int32)
    row_index = jnp.arange(tok_rows, dtype=jnp.int32)
    live_rows = row_index < tok_rows - lengths[0, lengths.shape[1] - 1]
    held_table = (placement[:, None] == expert_range).astype(jnp.int32)
    pair_range = jnp.arange(pair_count, dtype=jnp.int32)[:, None]
    first_pair = jnp.min(jnp.where(held_table > 0, pair_range, pair_count), axis=0)
    second_pair = jnp.max(jnp.where(held_table > 0, pair_range, -1), axis=0)
    upper_half = (row_index >= half_rows)[:, None, None]
    dest_table = jnp.where(upper_half, second_pair, first_pair)
    block_table = dest_table ^ own_pair
    match_table = expert_ids[:, :, None] == expert_range
    id_hot = match_table & live_rows[:, None, None]
    named = jnp.sum(id_hot.astype(jnp.float32), axis=1)
    before = (row_index[:, None] > row_index[None, :]) & (
        (row_index[:, None] >= half_rows) == (row_index[None, :] >= half_rows)
    )
    running = jnp.dot(
        before.astype(jnp.bfloat16), named.astype(jnp.bfloat16), preferred_element_type=jnp.float32
    ).astype(jnp.int32)
    slot_index = jnp.sum(
        jnp.where(id_hot, block_table * capacity + running[:, None, :], 0), axis=2
    )
    slot_index = jnp.where(live_rows[:, None], slot_index, pair_count * capacity)
    slot_range = jnp.arange(pair_count * capacity, dtype=jnp.int32)

    partial_out = jnp.dot(attn_heads, w_out, preferred_element_type=jnp.float32)
    state = residual_in.astype(jnp.float32) + core_scatter(partial_out)
    square_sum = core_sum(jnp.sum(state * state, axis=1, keepdims=True))
    inverse = lax.rsqrt(square_sum / full_width + epsilon)
    scaled = state * gain_attn
    normed_bf = (scaled * inverse).astype(jnp.bfloat16)

    logits = inverse * core_sum(
        jnp.dot(scaled, router.astype(jnp.float32), precision=lax.Precision.HIGHEST)
    )
    chosen = jnp.sum(match_table.astype(jnp.float32) * logits[:, None, :], axis=2)
    weights = jax.nn.sigmoid(chosen - chosen[:, ::-1])
    mix = jnp.where(slot_index[:, 0:1] == slot_range, weights[:, 0:1], 0.0) + jnp.where(
        slot_index[:, 1:2] == slot_range, weights[:, 1:2], 0.0
    )
    mix_high = lax.reduce_precision(mix, 8, 7)
    mix_low = (mix - mix_high).astype(jnp.bfloat16)
    mix_high = mix_high.astype(jnp.bfloat16)

    run = experts_of_two_cores if lax.axis_size("tp") == 2 else experts_of_any
    tables = (mix_high, mix_low)
    combined = run(slot_index.T, normed_bf, capacity, tables, state, w_gate_up, w_down, devices)
    final_sum = core_sum(jnp.sum(combined * combined, axis=1, keepdims=True))
    final_scale = lax.rsqrt(final_sum / full_width + epsilon)
    return (
        combined.astype(jnp.bfloat16),
        (combined * final_scale * gain_final).astype(jnp.bfloat16),
    )


def solution(mesh):
    placed = (
        P("req", "tp"),
        P("req", "tp"),
        P("tp", None),
        P("tp"),
        P("tp", None),
        P("req", None),
        P("req", None),
        P(),
        P("req", None, None, "tp"),
        P("req", "tp", None),
        P("tp"),
    )
    return jax.shard_map(
        on_device,
        mesh=mesh,
        in_specs=placed,
        out_specs=(P("req", "tp"), P("req", "tp")),
        check_vma=False,
    )
```

```python
import jax
import jax.numpy as jnp
from jax import lax
from jax.experimental import pallas as pl
from jax.experimental.pallas import tpu as pltpu
from jax.sharding import PartitionSpec as P

epsilon = 1e-05
UNITS = 256
LONG = 20_000_000_000
WHOLE = pl.BlockSpec(memory_space=pltpu.VMEM)
ANYWHERE = pl.BlockSpec(memory_space=pl.ANY)


def pair_shift(value, k, devices):
    return lax.ppermute(value, "req", [(i, 2 * ((i // 2) ^ k) + i % 2) for i in range(devices)])


def side_swap(value, devices):
    return lax.ppermute(value, "req", [(i, i ^ 1) for i in range(devices)])


def core_swap(value):
    return lax.ppermute(value, "tp", [(0, 1), (1, 0)])


def core_sum(value):
    if lax.axis_size("tp") == 2:
        return value + core_swap(value)
    return lax.psum(value, "tp")


def core_gather(value):
    if lax.axis_size("tp") != 2:
        return lax.all_gather(value, "tp", axis=1, tiled=True)
    other = core_swap(value)
    first = lax.axis_index("tp") == 0
    return jnp.concatenate([jnp.where(first, value, other), jnp.where(first, other, value)], axis=1)


def core_scatter(value):
    if lax.axis_size("tp") != 2:
        return lax.psum_scatter(
            value.astype(jnp.bfloat16), "tp", scatter_dimension=1, tiled=True
        ).astype(jnp.float32)
    width = value.shape[1] // 2
    first = lax.axis_index("tp") == 0
    low, high = value[:, :width], value[:, width:]
    away = jnp.where(first, high, low).astype(jnp.bfloat16)
    return jnp.where(first, low, high) + core_swap(away).astype(jnp.float32)


def slot_rows_kernel(blocks, slots_ref, rows_ref, *refs):
    slots = slots_ref[...]
    for out_ref, block in zip(refs[-len(blocks) :], blocks):
        shape = (out_ref.shape[0], slots.shape[1])
        here = lax.broadcasted_iota(jnp.int32, shape, 0) + block * shape[0]
        hot = jnp.where((slots[0:1] == here) | (slots[1:2] == here), 1.0, 0.0)
        out_ref[...] = jnp.dot(
            hot.astype(jnp.bfloat16), rows_ref[...], preferred_element_type=jnp.float32
        ).astype(jnp.bfloat16)


def slot_rows(blocks, capacity, slots, rows, after):
    outs = pl.pallas_call(
        lambda *refs: slot_rows_kernel(blocks, *refs),
        in_specs=[WHOLE, WHOLE] + [ANYWHERE] * len(after),
        out_specs=[WHOLE] * len(blocks),
        out_shape=[jax.ShapeDtypeStruct((capacity, rows.shape[1]), jnp.bfloat16)] * len(blocks),
        compiler_params=pltpu.CompilerParams(vmem_limit_bytes=16 << 20),
        name="slot_rows",
    )(slots, rows, *after)
    return dict(zip(blocks, outs))


def join_kernel(count, *refs):
    out_ref = refs[-1]
    start = 0
    for ref in refs[:count]:
        out_ref[start : start + ref.shape[0]] = ref[...]
        start += ref.shape[0]


def join(values, after, flops=0):
    rows = sum(value.shape[0] for value in values)
    return pl.pallas_call(
        lambda *refs: join_kernel(len(values), *refs),
        in_specs=[WHOLE] * len(values) + [ANYWHERE] * len(after),
        out_specs=WHOLE,
        out_shape=jax.ShapeDtypeStruct((rows, values[0].shape[1]), values[0].dtype),
        compiler_params=pltpu.CompilerParams(vmem_limit_bytes=16 << 20),
        cost_estimate=pl.CostEstimate(flops=flops, bytes_accessed=0, transcendentals=0),
        name="join",
    )(*values, *after)


def add_cores_kernel(counts, kept_ref, other_ref, *refs):
    outs = refs[-len(counts) - 1 :]
    start = outs[0].shape[0]
    outs[0][...] = kept_ref[:start] + other_ref[:start].astype(jnp.float32)
    for out_ref, count in zip(outs[1:], counts):
        part = slice(start, start + count)
        out_ref[...] = (kept_ref[part] + other_ref[part].astype(jnp.float32)).astype(jnp.bfloat16)
        start += count


def add_cores(kept, other, counts, after):
    rows, width = kept.shape
    return pl.pallas_call(
        lambda *refs: add_cores_kernel(counts, *refs),
        in_specs=[WHOLE, WHOLE] + [ANYWHERE] * len(after),
        out_specs=[WHOLE] * (len(counts) + 1),
        out_shape=[jax.ShapeDtypeStruct((rows - sum(counts), width), jnp.float32)]
        + [jax.ShapeDtypeStruct((count, width), jnp.bfloat16) for count in counts],
        compiler_params=pltpu.CompilerParams(vmem_limit_bytes=16 << 20),
        name="add_cores",
    )(kept, other, *after)


def add_sides_kernel(start, own_ref, other_ref, *refs):
    total = own_ref[start : start + other_ref.shape[0]] + other_ref[...].astype(jnp.float32)
    first = 0
    for out_ref in refs:
        out_ref[...] = total[first : first + out_ref.shape[0]].astype(jnp.bfloat16)
        first += out_ref.shape[0]


def add_sides(own, start, other, counts, after):
    return pl.pallas_call(
        lambda *refs: add_sides_kernel(start, *refs[:2], *refs[-len(counts) :]),
        in_specs=[WHOLE, WHOLE] + [ANYWHERE] * len(after),
        out_specs=[WHOLE] * len(counts),
        out_shape=[jax.ShapeDtypeStruct((n, own.shape[1]), jnp.bfloat16) for n in counts],
        compiler_params=pltpu.CompilerParams(vmem_limit_bytes=16 << 20),
        name="add_sides",
    )(own, other, *after)


def gate_up_kernel(counts, core_ref, *refs):
    pieces = refs[: 2 * len(counts)]
    weights_ref = refs[2 * len(counts)]
    out_ref, rows_ref = refs[-2:]
    width = pieces[0].shape[1]

    @pl.when(pl.program_id(0) == 0)
    def _():
        start = 0
        own = pl.multiple_of(core_ref[0] * width, width)
        other = pl.multiple_of((1 - core_ref[0]) * width, width)
        for i, count in enumerate(counts):
            rows_ref[start : start + count, pl.ds(own, width)] = pieces[2 * i][...]
            rows_ref[start : start + count, pl.ds(other, width)] = pieces[2 * i + 1][...]
            start += count

    rows = rows_ref[...]
    gate = jnp.dot(rows, weights_ref[0, 0], preferred_element_type=jnp.float32)
    up = jnp.dot(rows, weights_ref[0, 1], preferred_element_type=jnp.float32)
    out_ref[...] = (gate * jax.nn.sigmoid(gate) * up).astype(jnp.bfloat16)


def gate_up(core, pieces, weights, after, blocks=None):
    counts = [own.shape[0] for own, _ in pieces]
    rows = sum(counts)
    depth = weights.shape[2]
    block = UNITS
    first, last = blocks or (0, weights.shape[3] // block)
    units = (last - first) * block
    return pl.pallas_call(
        lambda *refs: gate_up_kernel(counts, *refs),
        grid_spec=pltpu.PrefetchScalarGridSpec(
            num_scalar_prefetch=1,
            grid=(units // block,),
            in_specs=[WHOLE] * (2 * len(counts))
            + [pl.BlockSpec((1, 2, depth, block), lambda i, core: (0, 0, 0, first + i))]
            + [ANYWHERE] * len(after),
            out_specs=pl.BlockSpec((rows, block), lambda i, core: (0, i)),
            scratch_shapes=[pltpu.VMEM((rows, depth), jnp.bfloat16)],
        ),
        out_shape=jax.ShapeDtypeStruct((rows, units), jnp.bfloat16),
        compiler_params=pltpu.CompilerParams(vmem_limit_bytes=36 << 20),
        cost_estimate=pl.CostEstimate(
            flops=rows * depth, bytes_accessed=depth, transcendentals=0
        ),
        name="gate_up",
    )(core, *[part for piece in pieces for part in piece], weights, *after)


def down_kernel(core_ref, activ_ref, weights_ref, *refs):
    out_ref = refs[-1]
    out_ref[...] = jnp.dot(
        activ_ref[...], weights_ref[0], preferred_element_type=jnp.float32
    ).astype(out_ref.dtype)


def down(core, activ, weights, away, after, flops=0):
    rows, units = activ.shape
    width = weights.shape[2] // 2
    block = 1024
    steps = width // block
    return pl.pallas_call(
        down_kernel,
        grid_spec=pltpu.PrefetchScalarGridSpec(
            num_scalar_prefetch=1,
            grid=(steps,),
            in_specs=[
                pl.BlockSpec((rows, units), lambda i, core: (0, 0)),
                pl.BlockSpec(
                    (1, units, block),
                    lambda i, core: (0, 0, (1 - core[0] if away else core[0]) * steps + i),
                ),
            ]
            + [ANYWHERE] * len(after),
            out_specs=pl.BlockSpec((rows, block), lambda i, core: (0, i)),
        ),
        out_shape=jax.ShapeDtypeStruct((rows, width), jnp.bfloat16 if away else jnp.float32),
        compiler_params=pltpu.CompilerParams(vmem_limit_bytes=44 << 20),
        cost_estimate=pl.CostEstimate(
            flops=flops or rows * units, bytes_accessed=units, transcendentals=0
        ),
        name="down_away" if away else "down_own",
    )(core, activ, weights, *after)


def down_both_kernel(count, core_ref, *refs):
    weights_ref = refs[count]
    away_ref, own_ref = refs[-2:]
    product, start = 0.0, 0
    for ref in refs[:count]:
        part = weights_ref[0, start : start + ref.shape[1]]
        product += jnp.dot(ref[...], part, preferred_element_type=jnp.float32)
        start += ref.shape[1]
    half = pl.num_programs(0) // 2

    @pl.when(pl.program_id(0) < half)
    def _():
        away_ref[...] = product.astype(jnp.bfloat16)

    @pl.when(pl.program_id(0) >= half)
    def _():
        own_ref[...] = product


def down_both(core, activ, weights, after):
    rows, units = activ[0].shape[0], weights.shape[1]
    width = weights.shape[2] // 2
    block = 1024
    half = width // block

    def columns(i, core):
        side = jnp.where(i < half, 1 - core[0], core[0])
        return (0, 0, side * half + lax.rem(i, half))

    return pl.pallas_call(
        lambda *refs: down_both_kernel(len(activ), *refs),
        grid_spec=pltpu.PrefetchScalarGridSpec(
            num_scalar_prefetch=1,
            grid=(2 * half,),
            in_specs=[
                pl.BlockSpec((rows, part.shape[1]), lambda i, core: (0, 0)) for part in activ
            ]
            + [pl.BlockSpec((1, units, block), columns)]
            + [ANYWHERE] * len(after),
            out_specs=[
                pl.BlockSpec((rows, block), lambda i, core: (0, jnp.minimum(i, half - 1))),
                pl.BlockSpec((rows, block), lambda i, core: (0, jnp.maximum(i - half, 0))),
            ],
        ),
        out_shape=[
            jax.ShapeDtypeStruct((rows, width), jnp.bfloat16),
            jax.ShapeDtypeStruct((rows, width), jnp.float32),
        ],
        compiler_params=pltpu.CompilerParams(vmem_limit_bytes=44 << 20),
        cost_estimate=pl.CostEstimate(flops=rows * units, bytes_accessed=units, transcendentals=0),
        name="down_both",
    )(core, *activ, weights, *after)


def mix_kernel(count, high_ref, low_ref, base_ref, *refs):
    out_ref = refs[-1]
    total = base_ref[...]
    width = high_ref.shape[1] // count
    for j, ref in enumerate(refs[:count]):
        part = slice(j * width, (j + 1) * width)
        total += jnp.dot(high_ref[:, part], ref[...], preferred_element_type=jnp.float32)
        total += jnp.dot(low_ref[:, part], ref[...], preferred_element_type=jnp.float32)
    out_ref[...] = total


def mix(tables, base, values, after, flops=0):
    return pl.pallas_call(
        lambda *refs: mix_kernel(len(values), *refs),
        in_specs=[WHOLE] * (3 + len(values)) + [ANYWHERE] * len(after),
        out_specs=WHOLE,
        out_shape=jax.ShapeDtypeStruct(base.shape, jnp.float32),
        compiler_params=pltpu.CompilerParams(vmem_limit_bytes=16 << 20),
        cost_estimate=pl.CostEstimate(flops=flops, bytes_accessed=0, transcendentals=0),
        name="mix",
    )(*tables, base, *values, *after)


def experts_of_two_cores(slots, rows, capacity, tables, state, w_gate_up, w_down, devices):
    pair_count = devices // 2
    core = lax.axis_index("tp").reshape(1)
    blocks = list(range(pair_count))
    quarter = pair_count // 4
    near, near_later, far, far_later = [
        blocks[i * quarter : (i + 1) * quarter] for i in range(4)
    ]
    size = quarter * capacity

    def columns(first):
        return [table[:, first * capacity : (first + quarter) * capacity] for table in tables]

    def send(group, values):
        return [pair_shift(x, k, devices) if k else x for k, x in zip(group, values)]

    outgoing = slot_rows(far + near + near_later, capacity, slots, rows, [])
    arrived = dict(zip(far, send(far, [outgoing[k] for k in far])))
    arrived |= zip(near, send(near, [outgoing[k] for k in near]))
    arrived |= zip(near_later, send(near_later, [outgoing[k] for k in near_later]))
    later = slot_rows(far_later, capacity, slots, rows, [arrived[near[-1]]])
    arrived |= zip(far_later, send(far_later, [later[k] for k in far_later]))

    spare = join([outgoing[near[0]]], [], LONG)
    near_own = join([arrived[k] for k in near], [])
    near_nbr = join([side_swap(near_own, devices)], [spare])
    far_own = join([arrived[k] for k in far], [near_nbr])
    spare = join([outgoing[near[0]]], [far_own], LONG)
    far_nbr = join([side_swap(far_own, devices)], [spare])
    near_later_own = join([arrived[k] for k in near_later], [near_nbr])
    near_later_nbr = side_swap(near_later_own, devices)

    pieces = [(x, core_swap(x)) for x in (far_own, near_own, far_nbr, near_nbr)]
    activ = gate_up(core, pieces, w_gate_up, [near_later_own])
    far_later_own = join([arrived[k] for k in far_later], [activ])
    far_later_nbr = side_swap(far_later_own, devices)
    near_later_nbr = join([near_later_nbr], [activ])
    away = down(core, activ, w_down, True, [far_later_own, near_later_nbr])
    far_later_nbr = join([far_later_nbr], [away])
    away = core_swap(away)
    kept = down(core, activ, w_down, False, [far_later_nbr], LONG)
    own, far_other, near_other = add_cores(kept, away, [size, size], [])
    pieces = [far_later_own, near_later_own, far_later_nbr, near_later_nbr]
    pieces = [(x, core_swap(x)) for x in pieces]
    unit_blocks = w_gate_up.shape[3] // UNITS
    split = unit_blocks // 2 + 1
    activ = [gate_up(core, pieces, w_gate_up, [own], (0, split))]

    far_other = side_swap(far_other, devices)
    near_other = side_swap(near_other, devices)
    totals = add_sides(own, 0, far_other, [capacity] * quarter, activ[:1])
    far_back = send(far, totals)
    activ.append(gate_up(core, pieces, w_gate_up, totals, (split, unit_blocks)))
    totals = add_sides(own, size, near_other, [capacity] * quarter, activ[1:])
    near_back = send(near, totals)
    away, kept = down_both(core, activ, w_down, totals)
    state = mix(columns(far[0]), state, far_back, [kept], LONG)
    state = mix(columns(near[0]), state, near_back, [])
    own, *others = add_cores(kept, core_swap(away), [capacity] * 2 * quarter, [state])
    back = []
    for j, k in enumerate(far_later + near_later):
        other = side_swap(others[j], devices)
        back += send([k], add_sides(own, j * capacity, other, [capacity], []))
    state = mix(columns(far_later[0]), state, back[:quarter], [], LONG)
    return mix(columns(near_later[0]), state, back[quarter:], [])


def experts_of_any(slots, rows, capacity, tables, state, w_gate_up, w_down, devices):
    pair_count = devices // 2
    slot_range = jnp.arange(pair_count * capacity, dtype=jnp.int32)[:, None]
    hot = ((slots[0:1] == slot_range) | (slots[1:2] == slot_range)).astype(jnp.bfloat16)
    outgoing = jnp.dot(hot, rows, preferred_element_type=jnp.float32).astype(jnp.bfloat16)
    outgoing = outgoing.reshape(pair_count, capacity, -1)
    own = [pair_shift(outgoing[k], k, devices) if k else outgoing[k] for k in range(pair_count)]
    own = jnp.concatenate(own, axis=0)
    rows = core_gather(jnp.concatenate([own, side_swap(own, devices)], axis=0))
    gate_proj = jnp.dot(rows, w_gate_up[0, 0], preferred_element_type=jnp.float32)
    up_proj = jnp.dot(rows, w_gate_up[0, 1], preferred_element_type=jnp.float32)
    activ = (jax.nn.silu(gate_proj) * up_proj).astype(jnp.bfloat16)
    reduced = core_scatter(jnp.dot(activ, w_down[0], preferred_element_type=jnp.float32))
    half = own.shape[0]
    swapped = side_swap(reduced[half:].astype(jnp.bfloat16), devices)
    total = (reduced[:half] + swapped.astype(jnp.float32)).astype(jnp.bfloat16)
    total = total.reshape(pair_count, capacity, -1)
    back = [pair_shift(total[k], k, devices) if k else total[k] for k in range(pair_count)]
    back = jnp.concatenate(back, axis=0)
    for table in tables:
        state += jnp.dot(table, back, preferred_element_type=jnp.float32)
    return state


def on_device(
    attn_heads,
    residual_in,
    w_out,
    gain_attn,
    router,
    expert_ids,
    lengths,
    placement,
    w_gate_up,
    w_down,
    gain_final,
):
    tok_rows = attn_heads.shape[0]
    half_rows = tok_rows // 2
    feat_width = residual_in.shape[1]
    full_width = feat_width * lax.axis_size("tp")
    devices = lax.axis_size("req")
    pair_count = devices // 2
    expert_count = devices // 4
    capacity = min(half_rows, 3 * tok_rows // (2 * expert_count))
    own_pair = lax.axis_index("req") // 2

    expert_range = jnp.arange(expert_count, dtype=jnp.int32)
    row_index = jnp.arange(tok_rows, dtype=jnp.int32)
    live_rows = row_index < tok_rows - lengths[0, lengths.shape[1] - 1]
    held_table = (placement[:, None] == expert_range).astype(jnp.int32)
    pair_range = jnp.arange(pair_count, dtype=jnp.int32)[:, None]
    first_pair = jnp.min(jnp.where(held_table > 0, pair_range, pair_count), axis=0)
    second_pair = jnp.max(jnp.where(held_table > 0, pair_range, -1), axis=0)
    upper_half = (row_index >= half_rows)[:, None, None]
    dest_table = jnp.where(upper_half, second_pair, first_pair)
    block_table = dest_table ^ own_pair
    match_table = expert_ids[:, :, None] == expert_range
    id_hot = match_table & live_rows[:, None, None]
    named = jnp.sum(id_hot.astype(jnp.float32), axis=1)
    before = (row_index[:, None] > row_index[None, :]) & (
        (row_index[:, None] >= half_rows) == (row_index[None, :] >= half_rows)
    )
    running = jnp.dot(
        before.astype(jnp.bfloat16), named.astype(jnp.bfloat16), preferred_element_type=jnp.float32
    ).astype(jnp.int32)
    slot_index = jnp.sum(
        jnp.where(id_hot, block_table * capacity + running[:, None, :], 0), axis=2
    )
    slot_index = jnp.where(live_rows[:, None], slot_index, pair_count * capacity)
    slot_range = jnp.arange(pair_count * capacity, dtype=jnp.int32)

    partial_out = jnp.dot(attn_heads, w_out, preferred_element_type=jnp.float32)
    state = residual_in.astype(jnp.float32) + core_scatter(partial_out)
    square_sum = core_sum(jnp.sum(state * state, axis=1, keepdims=True))
    inverse = lax.rsqrt(square_sum / full_width + epsilon)
    scaled = state * gain_attn
    normed_bf = (scaled * inverse).astype(jnp.bfloat16)

    logits = inverse * core_sum(
        jnp.dot(scaled, router.astype(jnp.float32), precision=lax.Precision.HIGHEST)
    )
    chosen = jnp.sum(match_table.astype(jnp.float32) * logits[:, None, :], axis=2)
    lead = chosen[:, 0:1] - chosen[:, 1:2]
    weights = jax.nn.sigmoid(jnp.concatenate([lead, -lead], axis=1))
    mix = jnp.where(slot_index[:, 0:1] == slot_range, weights[:, 0:1], 0.0) + jnp.where(
        slot_index[:, 1:2] == slot_range, weights[:, 1:2], 0.0
    )
    mix_high = lax.reduce_precision(mix, 8, 7)
    mix_low = (mix - mix_high).astype(jnp.bfloat16)
    mix_high = mix_high.astype(jnp.bfloat16)

    run = experts_of_two_cores if lax.axis_size("tp") == 2 else experts_of_any
    tables = (mix_high, mix_low)
    combined = run(slot_index.T, normed_bf, capacity, tables, state, w_gate_up, w_down, devices)
    final_sum = core_sum(jnp.sum(combined * combined, axis=1, keepdims=True))
    final_scale = lax.rsqrt(final_sum / full_width + epsilon)
    return (
        combined.astype(jnp.bfloat16),
        (combined * final_scale * gain_final).astype(jnp.bfloat16),
    )


def solution(mesh):
    placed = (
        P("req", "tp"),
        P("req", "tp"),
        P("tp", None),
        P("tp"),
        P("tp", None),
        P("req", None),
        P("req", None),
        P(),
        P("req", None, None, "tp"),
        P("req", "tp", None),
        P("tp"),
    )
    return jax.shard_map(
        on_device,
        mesh=mesh,
        in_specs=placed,
        out_specs=(P("req", "tp"), P("req", "tp")),
        check_vma=False,
    )
```

```python
import jax
import jax.numpy as jnp
from jax import lax
from jax.experimental import pallas as pl
from jax.experimental.pallas import tpu as pltpu
from jax.sharding import PartitionSpec as P

epsilon = 1e-05
UNITS = 256
LONG = 20_000_000_000
WHOLE = pl.BlockSpec(memory_space=pltpu.VMEM)
ANYWHERE = pl.BlockSpec(memory_space=pl.ANY)


def pair_shift(value, k, devices):
    return lax.ppermute(value, "req", [(i, 2 * ((i // 2) ^ k) + i % 2) for i in range(devices)])


def side_swap(value, devices):
    return lax.ppermute(value, "req", [(i, i ^ 1) for i in range(devices)])


def core_swap(value):
    return lax.ppermute(value, "tp", [(0, 1), (1, 0)])


def core_sum(value):
    if lax.axis_size("tp") == 2:
        return value + core_swap(value)
    return lax.psum(value, "tp")


def core_gather(value):
    if lax.axis_size("tp") != 2:
        return lax.all_gather(value, "tp", axis=1, tiled=True)
    other = core_swap(value)
    first = lax.axis_index("tp") == 0
    return jnp.concatenate([jnp.where(first, value, other), jnp.where(first, other, value)], axis=1)


def core_scatter(value):
    if lax.axis_size("tp") != 2:
        return lax.psum_scatter(
            value.astype(jnp.bfloat16), "tp", scatter_dimension=1, tiled=True
        ).astype(jnp.float32)
    width = value.shape[1] // 2
    first = lax.axis_index("tp") == 0
    low, high = value[:, :width], value[:, width:]
    away = jnp.where(first, high, low).astype(jnp.bfloat16)
    return jnp.where(first, low, high) + core_swap(away).astype(jnp.float32)


def slot_rows_kernel(blocks, slots_ref, rows_ref, *refs):
    slots = slots_ref[...]
    for out_ref, block in zip(refs[-len(blocks) :], blocks):
        shape = (out_ref.shape[0], slots.shape[1])
        here = lax.broadcasted_iota(jnp.int32, shape, 0) + block * shape[0]
        hot = jnp.where((slots[0:1] == here) | (slots[1:2] == here), 1.0, 0.0)
        out_ref[...] = jnp.dot(
            hot.astype(jnp.bfloat16), rows_ref[...], preferred_element_type=jnp.float32
        ).astype(jnp.bfloat16)


def slot_rows(blocks, capacity, slots, rows, after):
    outs = pl.pallas_call(
        lambda *refs: slot_rows_kernel(blocks, *refs),
        in_specs=[WHOLE, WHOLE] + [ANYWHERE] * len(after),
        out_specs=[WHOLE] * len(blocks),
        out_shape=[jax.ShapeDtypeStruct((capacity, rows.shape[1]), jnp.bfloat16)] * len(blocks),
        compiler_params=pltpu.CompilerParams(vmem_limit_bytes=16 << 20),
        name="slot_rows",
    )(slots, rows, *after)
    return dict(zip(blocks, outs))


def join_kernel(count, *refs):
    out_ref = refs[-1]
    start = 0
    for ref in refs[:count]:
        out_ref[start : start + ref.shape[0]] = ref[...]
        start += ref.shape[0]


def join(values, after, flops=0):
    rows = sum(value.shape[0] for value in values)
    return pl.pallas_call(
        lambda *refs: join_kernel(len(values), *refs),
        in_specs=[WHOLE] * len(values) + [ANYWHERE] * len(after),
        out_specs=WHOLE,
        out_shape=jax.ShapeDtypeStruct((rows, values[0].shape[1]), values[0].dtype),
        compiler_params=pltpu.CompilerParams(vmem_limit_bytes=16 << 20),
        cost_estimate=pl.CostEstimate(flops=flops, bytes_accessed=0, transcendentals=0),
        name="join",
    )(*values, *after)


def add_cores_kernel(counts, kept_ref, other_ref, *refs):
    outs = refs[-len(counts) - 1 :]
    start = outs[0].shape[0]
    outs[0][...] = kept_ref[:start] + other_ref[:start].astype(jnp.float32)
    for out_ref, count in zip(outs[1:], counts):
        part = slice(start, start + count)
        out_ref[...] = (kept_ref[part] + other_ref[part].astype(jnp.float32)).astype(jnp.bfloat16)
        start += count


def add_cores(kept, other, counts, after):
    rows, width = kept.shape
    return pl.pallas_call(
        lambda *refs: add_cores_kernel(counts, *refs),
        in_specs=[WHOLE, WHOLE] + [ANYWHERE] * len(after),
        out_specs=[WHOLE] * (len(counts) + 1),
        out_shape=[jax.ShapeDtypeStruct((rows - sum(counts), width), jnp.float32)]
        + [jax.ShapeDtypeStruct((count, width), jnp.bfloat16) for count in counts],
        compiler_params=pltpu.CompilerParams(vmem_limit_bytes=16 << 20),
        name="add_cores",
    )(kept, other, *after)


def add_sent_kernel(kept_ref, other_ref, *refs):
    count = len(refs)
    start = kept_ref.shape[0] - other_ref.shape[0]
    step = other_ref.shape[0] // count
    for j, out_ref in enumerate(refs):
        part = kept_ref[start + j * step : start + (j + 1) * step]
        part += other_ref[j * step : (j + 1) * step].astype(jnp.float32)
        out_ref[...] = part.astype(jnp.bfloat16)


def add_sent(kept, other, count, after):
    rows, width = other.shape
    return pl.pallas_call(
        lambda *refs: add_sent_kernel(*refs[:2], *refs[-count:]),
        in_specs=[WHOLE, WHOLE] + [ANYWHERE] * len(after),
        out_specs=[WHOLE] * count,
        out_shape=[jax.ShapeDtypeStruct((rows // count, width), jnp.bfloat16)] * count,
        compiler_params=pltpu.CompilerParams(vmem_limit_bytes=16 << 20),
        name="add_sent",
    )(kept, other, *after)


def add_sides_kernel(start, own_ref, other_ref, *refs):
    total = own_ref[start : start + other_ref.shape[0]] + other_ref[...].astype(jnp.float32)
    first = 0
    for out_ref in refs:
        out_ref[...] = total[first : first + out_ref.shape[0]].astype(jnp.bfloat16)
        first += out_ref.shape[0]


def add_sides(own, start, other, counts, after):
    return pl.pallas_call(
        lambda *refs: add_sides_kernel(start, *refs[:2], *refs[-len(counts) :]),
        in_specs=[WHOLE, WHOLE] + [ANYWHERE] * len(after),
        out_specs=[WHOLE] * len(counts),
        out_shape=[jax.ShapeDtypeStruct((n, own.shape[1]), jnp.bfloat16) for n in counts],
        compiler_params=pltpu.CompilerParams(vmem_limit_bytes=16 << 20),
        name="add_sides",
    )(own, other, *after)


def gate_up_kernel(counts, core_ref, *refs):
    pieces = refs[: 2 * len(counts)]
    weights_ref = refs[2 * len(counts)]
    out_ref, rows_ref = refs[-2:]
    width = pieces[0].shape[1]

    @pl.when(pl.program_id(0) == 0)
    def _():
        start = 0
        own = pl.multiple_of(core_ref[0] * width, width)
        other = pl.multiple_of((1 - core_ref[0]) * width, width)
        for i, count in enumerate(counts):
            rows_ref[start : start + count, pl.ds(own, width)] = pieces[2 * i][...]
            rows_ref[start : start + count, pl.ds(other, width)] = pieces[2 * i + 1][...]
            start += count

    rows = rows_ref[...]
    gate = jnp.dot(rows, weights_ref[0, 0], preferred_element_type=jnp.float32)
    up = jnp.dot(rows, weights_ref[0, 1], preferred_element_type=jnp.float32)
    out_ref[...] = (gate * jax.nn.sigmoid(gate) * up).astype(jnp.bfloat16)


def gate_up(core, pieces, weights, after, blocks=None):
    counts = [own.shape[0] for own, _ in pieces]
    rows = sum(counts)
    depth = weights.shape[2]
    block = UNITS
    first, last = blocks or (0, weights.shape[3] // block)
    units = (last - first) * block
    return pl.pallas_call(
        lambda *refs: gate_up_kernel(counts, *refs),
        grid_spec=pltpu.PrefetchScalarGridSpec(
            num_scalar_prefetch=1,
            grid=(units // block,),
            in_specs=[WHOLE] * (2 * len(counts))
            + [pl.BlockSpec((1, 2, depth, block), lambda i, core: (0, 0, 0, first + i))]
            + [ANYWHERE] * len(after),
            out_specs=pl.BlockSpec((rows, block), lambda i, core: (0, i)),
            scratch_shapes=[pltpu.VMEM((rows, depth), jnp.bfloat16)],
        ),
        out_shape=jax.ShapeDtypeStruct((rows, units), jnp.bfloat16),
        compiler_params=pltpu.CompilerParams(vmem_limit_bytes=36 << 20),
        cost_estimate=pl.CostEstimate(
            flops=rows * depth, bytes_accessed=depth, transcendentals=0
        ),
        name="gate_up",
    )(core, *[part for piece in pieces for part in piece], weights, *after)


def down_both_kernel(count, core_ref, *refs):
    weights_ref = refs[count]
    away_ref, send_ref, own_ref = refs[-3:]
    keep = away_ref.shape[0]
    product, start = 0.0, 0
    for ref in refs[:count]:
        part = weights_ref[0, start : start + ref.shape[1]]
        product += jnp.dot(ref[...], part, preferred_element_type=jnp.float32)
        start += ref.shape[1]
    half = pl.num_programs(0) // 2

    @pl.when(pl.program_id(0) < half)
    def _():
        away_ref[...] = product[:keep].astype(jnp.bfloat16)
        send_ref[...] = product[keep:].astype(jnp.bfloat16)

    @pl.when(pl.program_id(0) >= half)
    def _():
        own_ref[...] = product


def down_both(core, activ, weights, after):
    rows, units = activ[0].shape[0], weights.shape[1]
    width = weights.shape[2] // 2
    block = 1024
    half = width // block

    def columns(i, core):
        side = jnp.where(i < half, 1 - core[0], core[0])
        return (0, 0, side * half + lax.rem(i, half))

    return pl.pallas_call(
        lambda *refs: down_both_kernel(len(activ), *refs),
        grid_spec=pltpu.PrefetchScalarGridSpec(
            num_scalar_prefetch=1,
            grid=(2 * half,),
            in_specs=[
                pl.BlockSpec((rows, part.shape[1]), lambda i, core: (0, 0)) for part in activ
            ]
            + [pl.BlockSpec((1, units, block), columns)]
            + [ANYWHERE] * len(after),
            out_specs=[
                pl.BlockSpec((rows // 2, block), lambda i, core: (0, jnp.minimum(i, half - 1))),
                pl.BlockSpec((rows // 2, block), lambda i, core: (0, jnp.minimum(i, half - 1))),
                pl.BlockSpec((rows, block), lambda i, core: (0, jnp.maximum(i - half, 0))),
            ],
        ),
        out_shape=[
            jax.ShapeDtypeStruct((rows // 2, width), jnp.bfloat16),
            jax.ShapeDtypeStruct((rows // 2, width), jnp.bfloat16),
            jax.ShapeDtypeStruct((rows, width), jnp.float32),
        ],
        compiler_params=pltpu.CompilerParams(vmem_limit_bytes=44 << 20),
        cost_estimate=pl.CostEstimate(flops=rows * units, bytes_accessed=units, transcendentals=0),
        name="down_both",
    )(core, *activ, weights, *after)


def mix_kernel(count, high_ref, low_ref, base_ref, *refs):
    out_ref = refs[-1]
    total = base_ref[...]
    width = high_ref.shape[1] // count
    for j, ref in enumerate(refs[:count]):
        part = slice(j * width, (j + 1) * width)
        total += jnp.dot(high_ref[:, part], ref[...], preferred_element_type=jnp.float32)
        total += jnp.dot(low_ref[:, part], ref[...], preferred_element_type=jnp.float32)
    out_ref[...] = total


def mix(tables, base, values, after, flops=0):
    return pl.pallas_call(
        lambda *refs: mix_kernel(len(values), *refs),
        in_specs=[WHOLE] * (3 + len(values)) + [ANYWHERE] * len(after),
        out_specs=WHOLE,
        out_shape=jax.ShapeDtypeStruct(base.shape, jnp.float32),
        compiler_params=pltpu.CompilerParams(vmem_limit_bytes=16 << 20),
        cost_estimate=pl.CostEstimate(flops=flops, bytes_accessed=0, transcendentals=0),
        name="mix",
    )(*tables, base, *values, *after)


def experts_of_two_cores(slots, rows, capacity, tables, state, w_gate_up, w_down, devices):
    pair_count = devices // 2
    core = lax.axis_index("tp").reshape(1)
    blocks = list(range(pair_count))
    quarter = pair_count // 4
    near, near_later, far, far_later = [
        blocks[i * quarter : (i + 1) * quarter] for i in range(4)
    ]
    size = quarter * capacity

    def columns(first):
        return [table[:, first * capacity : (first + quarter) * capacity] for table in tables]

    def send(group, values):
        return [pair_shift(x, k, devices) if k else x for k, x in zip(group, values)]

    outgoing = slot_rows(far + near + near_later, capacity, slots, rows, [])
    arrived = dict(zip(far, send(far, [outgoing[k] for k in far])))
    arrived |= zip(near, send(near, [outgoing[k] for k in near]))
    arrived |= zip(near_later, send(near_later, [outgoing[k] for k in near_later]))
    later = slot_rows(far_later, capacity, slots, rows, [arrived[near[-1]]])
    arrived |= zip(far_later, send(far_later, [later[k] for k in far_later]))

    spare = join([outgoing[near[0]]], [], LONG)
    near_own = join([arrived[k] for k in near], [])
    near_nbr = join([side_swap(near_own, devices)], [spare])
    far_own = join([arrived[k] for k in far], [near_nbr])
    spare = join([outgoing[near[0]]], [far_own], LONG)
    far_nbr = join([side_swap(far_own, devices)], [spare])
    near_later_own = join([arrived[k] for k in near_later], [near_nbr])
    near_later_nbr = side_swap(near_later_own, devices)

    pieces = [(x, core_swap(x)) for x in (far_own, near_own, far_nbr, near_nbr)]
    activ = gate_up(core, pieces, w_gate_up, [near_later_own])
    far_later_own = join([arrived[k] for k in far_later], [activ])
    far_later_nbr = side_swap(far_later_own, devices)
    near_later_nbr = join([near_later_nbr], [activ])
    away, sent, kept = down_both(core, [activ], w_down, [far_later_own, near_later_nbr])
    far_later_nbr = join([far_later_nbr], [kept], LONG)
    far_other, near_other = add_sent(kept, core_swap(sent), 2, [far_later_nbr])
    (own,) = add_cores(kept[: 2 * size], core_swap(away), [], [far_other])
    pieces = [far_later_own, near_later_own, far_later_nbr, near_later_nbr]
    pieces = [(x, core_swap(x)) for x in pieces]
    unit_blocks = w_gate_up.shape[3] // UNITS
    split = unit_blocks // 2 + 1
    activ = [gate_up(core, pieces, w_gate_up, [own], (0, split))]

    far_other = side_swap(far_other, devices)
    near_other = side_swap(near_other, devices)
    totals = add_sides(own, 0, far_other, [capacity] * quarter, activ[:1])
    far_back = send(far, totals)
    activ.append(gate_up(core, pieces, w_gate_up, totals, (split, unit_blocks)))
    totals = add_sides(own, size, near_other, [capacity] * quarter, activ[1:])
    near_back = send(near, totals)
    away, sent, kept = down_both(core, activ, w_down, totals)
    state = mix(columns(far[0]), state, far_back, [kept], LONG)
    state = mix(columns(near[0]), state, near_back, [])
    others = add_sent(kept, core_swap(sent), 2 * quarter, [state])
    (own,) = add_cores(kept[: 2 * size], core_swap(away), [], [others[0]])
    back = []
    for j, k in enumerate(far_later + near_later):
        other = side_swap(others[j], devices)
        back += send([k], add_sides(own, j * capacity, other, [capacity], []))
    state = mix(columns(far_later[0]), state, back[:quarter], [], LONG)
    return mix(columns(near_later[0]), state, back[quarter:], [])


def experts_of_any(slots, rows, capacity, tables, state, w_gate_up, w_down, devices):
    pair_count = devices // 2
    slot_range = jnp.arange(pair_count * capacity, dtype=jnp.int32)[:, None]
    hot = ((slots[0:1] == slot_range) | (slots[1:2] == slot_range)).astype(jnp.bfloat16)
    outgoing = jnp.dot(hot, rows, preferred_element_type=jnp.float32).astype(jnp.bfloat16)
    outgoing = outgoing.reshape(pair_count, capacity, -1)
    own = [pair_shift(outgoing[k], k, devices) if k else outgoing[k] for k in range(pair_count)]
    own = jnp.concatenate(own, axis=0)
    rows = core_gather(jnp.concatenate([own, side_swap(own, devices)], axis=0))
    gate_proj = jnp.dot(rows, w_gate_up[0, 0], preferred_element_type=jnp.float32)
    up_proj = jnp.dot(rows, w_gate_up[0, 1], preferred_element_type=jnp.float32)
    activ = (jax.nn.silu(gate_proj) * up_proj).astype(jnp.bfloat16)
    reduced = core_scatter(jnp.dot(activ, w_down[0], preferred_element_type=jnp.float32))
    half = own.shape[0]
    swapped = side_swap(reduced[half:].astype(jnp.bfloat16), devices)
    total = (reduced[:half] + swapped.astype(jnp.float32)).astype(jnp.bfloat16)
    total = total.reshape(pair_count, capacity, -1)
    back = [pair_shift(total[k], k, devices) if k else total[k] for k in range(pair_count)]
    back = jnp.concatenate(back, axis=0)
    for table in tables:
        state += jnp.dot(table, back, preferred_element_type=jnp.float32)
    return state


def on_device(
    attn_heads,
    residual_in,
    w_out,
    gain_attn,
    router,
    expert_ids,
    lengths,
    placement,
    w_gate_up,
    w_down,
    gain_final,
):
    tok_rows = attn_heads.shape[0]
    half_rows = tok_rows // 2
    feat_width = residual_in.shape[1]
    full_width = feat_width * lax.axis_size("tp")
    devices = lax.axis_size("req")
    pair_count = devices // 2
    expert_count = devices // 4
    capacity = min(half_rows, 3 * tok_rows // (2 * expert_count))
    own_pair = lax.axis_index("req") // 2

    expert_range = jnp.arange(expert_count, dtype=jnp.int32)
    row_index = jnp.arange(tok_rows, dtype=jnp.int32)
    live_rows = row_index < tok_rows - lengths[0, lengths.shape[1] - 1]
    held_table = (placement[:, None] == expert_range).astype(jnp.int32)
    pair_range = jnp.arange(pair_count, dtype=jnp.int32)[:, None]
    first_pair = jnp.min(jnp.where(held_table > 0, pair_range, pair_count), axis=0)
    second_pair = jnp.max(jnp.where(held_table > 0, pair_range, -1), axis=0)
    upper_half = (row_index >= half_rows)[:, None, None]
    dest_table = jnp.where(upper_half, second_pair, first_pair)
    block_table = dest_table ^ own_pair
    match_table = expert_ids[:, :, None] == expert_range
    id_hot = match_table & live_rows[:, None, None]
    named = jnp.sum(id_hot.astype(jnp.float32), axis=1)
    before = (row_index[:, None] > row_index[None, :]) & (
        (row_index[:, None] >= half_rows) == (row_index[None, :] >= half_rows)
    )
    running = jnp.dot(
        before.astype(jnp.bfloat16), named.astype(jnp.bfloat16), preferred_element_type=jnp.float32
    ).astype(jnp.int32)
    slot_index = jnp.sum(
        jnp.where(id_hot, block_table * capacity + running[:, None, :], 0), axis=2
    )
    slot_index = jnp.where(live_rows[:, None], slot_index, pair_count * capacity)
    slot_range = jnp.arange(pair_count * capacity, dtype=jnp.int32)

    partial_out = jnp.dot(attn_heads, w_out, preferred_element_type=jnp.float32)
    state = residual_in.astype(jnp.float32) + core_scatter(partial_out)
    square_sum = core_sum(jnp.sum(state * state, axis=1, keepdims=True))
    inverse = lax.rsqrt(square_sum / full_width + epsilon)
    scaled = state * gain_attn
    normed_bf = (scaled * inverse).astype(jnp.bfloat16)

    logits = inverse * core_sum(
        jnp.dot(scaled, router.astype(jnp.float32), precision=lax.Precision.HIGHEST)
    )
    chosen = jnp.sum(match_table.astype(jnp.float32) * logits[:, None, :], axis=2)
    lead = chosen[:, 0:1] - chosen[:, 1:2]
    weights = jax.nn.sigmoid(jnp.concatenate([lead, -lead], axis=1))
    mix = jnp.where(slot_index[:, 0:1] == slot_range, weights[:, 0:1], 0.0) + jnp.where(
        slot_index[:, 1:2] == slot_range, weights[:, 1:2], 0.0
    )
    mix_high = lax.reduce_precision(mix, 8, 7)
    mix_low = (mix - mix_high).astype(jnp.bfloat16)
    mix_high = mix_high.astype(jnp.bfloat16)

    run = experts_of_two_cores if lax.axis_size("tp") == 2 else experts_of_any
    tables = (mix_high, mix_low)
    combined = run(slot_index.T, normed_bf, capacity, tables, state, w_gate_up, w_down, devices)
    final_sum = core_sum(jnp.sum(combined * combined, axis=1, keepdims=True))
    final_scale = lax.rsqrt(final_sum / full_width + epsilon)
    return (
        combined.astype(jnp.bfloat16),
        (combined * final_scale * gain_final).astype(jnp.bfloat16),
    )


def solution(mesh):
    placed = (
        P("req", "tp"),
        P("req", "tp"),
        P("tp", None),
        P("tp"),
        P("tp", None),
        P("req", None),
        P("req", None),
        P(),
        P("req", None, None, "tp"),
        P("req", "tp", None),
        P("tp"),
    )
    return jax.shard_map(
        on_device,
        mesh=mesh,
        in_specs=placed,
        out_specs=(P("req", "tp"), P("req", "tp")),
        check_vma=False,
    )
```
